32 devices in a mesh: slab: 8 (over z, y), disk: 4 (over x, core).
Axes of the slice: x: 2, y: 2, z: 4, core: 2. Of those that a mesh axis runs over, the one named last changes fastest.
Arguments:
- thermal_anomaly: float32 [2, 8, 1024], P(None, 'slab', 'disk'), may hold values from 0.5 to 1.5
- humidity_amount: float32 [2, 8, 1024], P(None, 'slab', 'disk'), may hold values from 0.2 to 2
- slab_condensate_amount: float32 [2, 8, 1024], P(None, 'slab', 'disk'), may hold values from 0.1 to 2
- overcast_indicator: int32 [2, 1024], P(None, 'disk'), may hold values 0 or 1
- molecular_opacity: float32 [112, 8], replicated, may hold values from 0.003 to 0.1
- condensate_opacity: float32 [112], replicated, may hold values from 0.01 to 0.1
- planck_quadrature_factor: float32 [112], replicated, may hold values from 0.5 to 2
- scene_contributing_profiles: int32 [4, 16384], P(None, ('slab', 'disk')), may hold values from 0 to 1023, as said below
- scene_interpolation_factors: float32 [4, 16384], P(None, ('slab', 'disk')), may hold values from 0.1 to 1
Outputs:
- pixel_radiance: float32 [2, 16, 16384], P(None, None, ('slab', 'disk'))
The draws below stay inside these ranges and needn't reach their ends.
Inputs may be any that keep to these rules, and one draw needn't show every extreme that they name: `scene_contributing_profiles`: every source column c of pixel p lies in the pixel's latitude strip: (c % 256) // 32 == p // 2048.
All inputs are finite; a program needn't handle non-finite values. No bound on the sum of `overcast_indicator` on one device may be relied on, other than what follows from the above.
Results may differ from the reference program's by a relative error of at most 0.0017.
Values may be sent and summed in bfloat16 or wider, within the bound.
A program may use at most 64 MiB of HBM per device.

```python
import math
import jax
import jax.numpy as jnp
from jax import lax

COLS_DEV = 32
RESULT_TIMES = 2
G = 112
BANDS = 16
TAPS = 4
GPB = 7
VERTICAL_STEPS = 8
STRIP = 256
GRID_PROFILES = 1024
PIX_ROW = 2048
PIXELS = 16384
N_DISK = 4


def draw_scene_contributing_profiles(key, part):
    key_owner, key_within = jax.random.split(key, 2)
    strip_row = jnp.arange(PIXELS) // PIX_ROW
    sector = jax.random.randint(key_owner, (TAPS, PIXELS), 0, N_DISK)
    within = jax.random.randint(key_within, (TAPS, PIXELS), 0, COLS_DEV)
    return (sector * STRIP + strip_row[None, :] * COLS_DEV + within).astype(jnp.int32)


def plant(entries, stream_key, smallest, top_value):
    spot = [jax.random.randint(jax.random.fold_in(stream_key, axis), (), 0, length) for axis, length in enumerate(entries.shape)]
    longest = entries.shape.index(max(entries.shape))
    neighbour = spot[:longest] + [(spot[longest] + 1) % entries.shape[longest]] + spot[longest + 1:]
    return entries.at[tuple(spot)].set(smallest).at[tuple(neighbour)].set(top_value)


def steps_of(stream_key, dims, cuts, smallest, top_value):
    level = 1.0
    for position, blocks in cuts:
        heights = jax.random.uniform(jax.random.fold_in(jax.random.fold_in(stream_key, 6), position), (blocks,), jnp.float32, smallest / len(cuts), top_value / len(cuts))
        level = level * jnp.repeat(jnp.exp(heights), dims[position] // blocks).reshape((-1,) + (1,) * (len(dims) - 1 - position))
    return level


def setup_inputs(seed: int = 0) -> dict:
    key_list = jax.random.split(jax.random.key(seed), 10)
    thermal_anomaly = jnp.clip(0.5 + 1.0 * jax.random.uniform(key_list[0], (RESULT_TIMES, VERTICAL_STEPS, GRID_PROFILES), jnp.float32) ** steps_of(key_list[0], (RESULT_TIMES, VERTICAL_STEPS, GRID_PROFILES), ((1, 8), (2, 4)), -0.2, 0.2), 0.5, 1.5)
    humidity_amount = jnp.clip(jnp.exp(math.log(2.0) - 2.3025851 * jax.random.uniform(key_list[1], (RESULT_TIMES, VERTICAL_STEPS, GRID_PROFILES), jnp.float32) ** steps_of(key_list[1], (RESULT_TIMES, VERTICAL_STEPS, GRID_PROFILES), ((1, 8), (2, 4)), -0.2, 0.2)), 0.2, 2.0)
    slab_condensate_amount = jnp.clip(jnp.exp(math.log(2.0) - 2.9957323 * jax.random.uniform(key_list[2], (RESULT_TIMES, VERTICAL_STEPS, GRID_PROFILES), jnp.float32) ** steps_of(key_list[2], (RESULT_TIMES, VERTICAL_STEPS, GRID_PROFILES), ((1, 8), (2, 4)), -0.2, 0.2)), 0.1, 2.0)
    overcast_indicator = plant((jax.random.randint(key_list[3], (RESULT_TIMES, GRID_PROFILES), 0, 2) < 1).astype(jnp.int32), jax.random.fold_in(key_list[3], 1), 0, 1)
    molecular_opacity = jnp.clip(jnp.exp(jax.random.uniform(key_list[4], (G, VERTICAL_STEPS), jnp.float32, math.log(0.003), math.log(0.1))), 0.003, 0.1)
    condensate_opacity = jnp.clip(jnp.exp(jax.random.uniform(key_list[5], (G,), jnp.float32, math.log(0.01), math.log(0.1))), 0.01, 0.1)
    planck_quadrature_factor = jnp.clip(jnp.exp(jax.random.uniform(key_list[6], (G,), jnp.float32, math.log(0.5), math.log(2.0))), 0.5, 2.0)
    scene_contributing_profiles = draw_scene_contributing_profiles(jax.random.fold_in(key_list[9], 71), 0)
    scene_interpolation_factors = jnp.clip(0.1 + 0.9 * jax.random.uniform(key_list[8], (TAPS, PIXELS), jnp.float32) ** steps_of(key_list[8], (TAPS, PIXELS), ((1, 32),), -0.2, 0.2), 0.1, 1.0)
    return {"thermal_anomaly": thermal_anomaly, "humidity_amount": humidity_amount, "slab_condensate_amount": slab_condensate_amount, "overcast_indicator": overcast_indicator, "molecular_opacity": molecular_opacity, "condensate_opacity": condensate_opacity, "planck_quadrature_factor": planck_quadrature_factor, "scene_contributing_profiles": scene_contributing_profiles, "scene_interpolation_factors": scene_interpolation_factors}


def band_block(temp_four, vapour_cols, cloud_cols, gas_band, cloud_band, planck_band):
    optical_depth = gas_band[:, :, None] * vapour_cols[None] + cloud_band[:, None, None] * cloud_cols[None]
    optical_depth_above = jnp.cumsum(optical_depth, axis=1) - optical_depth
    planck = planck_band[:, None, None] * temp_four[None]
    visible = jnp.exp(-optical_depth_above)
    emitted = jnp.sum(planck * visible * (1.0 - jnp.exp(-optical_depth)), axis=1)
    ground = planck[:, -1] * visible[:, -1] * jnp.exp(-optical_depth[:, -1])
    return jnp.sum(emitted + ground, axis=0) / gas_band.shape[0]


def radiate(temp_cols, vapour_cols, cloud_cols, molecular_opacity, condensate_opacity, planck_quadrature_factor):
    temp_four = temp_cols ** 4
    gas_bands = molecular_opacity.reshape(BANDS, GPB, VERTICAL_STEPS)
    cloud_bands = condensate_opacity.reshape(BANDS, GPB)
    planck_bands = planck_quadrature_factor.reshape(BANDS, GPB)

    def one_band(pieces):
        return band_block(temp_four, vapour_cols, cloud_cols, pieces[0], pieces[1], pieces[2])

    return lax.map(one_band, (gas_bands, cloud_bands, planck_bands))


def reference(thermal_anomaly, humidity_amount, slab_condensate_amount, overcast_indicator, molecular_opacity, condensate_opacity, planck_quadrature_factor, scene_contributing_profiles, scene_interpolation_factors):
    overcast_fraction_intensity = slab_condensate_amount * overcast_indicator.astype(jnp.float32)[:, None, :]
    blocks = GRID_PROFILES // COLS_DEV
    results = []
    for hour in range(RESULT_TIMES):
        def collect_profiles_again(field):
            return field[hour].reshape(VERTICAL_STEPS, blocks, COLS_DEV).transpose(1, 0, 2)

        def lone_partition(pieces):
            return radiate(pieces[0], pieces[1], pieces[2], molecular_opacity, condensate_opacity, planck_quadrature_factor)

        spectral_interval_intensity = lax.map(lone_partition, (collect_profiles_again(thermal_anomaly), collect_profiles_again(humidity_amount), collect_profiles_again(overcast_fraction_intensity)))
        spectral_interval_intensity = spectral_interval_intensity.transpose(1, 0, 2).reshape(BANDS, GRID_PROFILES).astype(jnp.bfloat16)
        picked = spectral_interval_intensity[:, scene_contributing_profiles].astype(jnp.float32)
        results.append(jnp.sum(picked * scene_interpolation_factors[None], axis=1))
    return jnp.stack(results)
```

```python
import functools

import jax
import jax.numpy as jnp
from jax import lax
from jax.experimental import pallas as pl
from jax.experimental.pallas import tpu as pltpu
from jax.sharding import PartitionSpec as P

BANDS = 16
GPB = 7
LANES = 128
MESH = pl.DeviceIdType.MESH
NEG_LOG2E = -1.4426950408889634


def loop(count, body):
    if count <= 64:
        for i in range(count):
            body(i)
    else:
        lax.fori_loop(0, count, lambda i, _: (body(i), 0)[1], 0)


def kernel(
    n_slab, n_disk, sector_cols, block_cols,
    t_hbm, q_hbm, c_hbm, o_hbm, mol_hbm, cond_hbm, pf_hbm, src_hbm, w_hbm,
    out_ref,
    t_ref, q_ref, c_ref, o_ref, mol_ref, cond_ref, pf_ref, src_ref, w_ref,
    fld, pk, recv, sel, mb, cb, pb, whi, wlo,
    in_sems, send_sem, recv_sem,
):
    n = n_slab * n_disk
    levels = n_slab
    halves = sector_cols // LANES
    per = LANES // block_cols
    me_s = lax.axis_index("slab")
    me_d = lax.axis_index("disk")
    me = me_s * n_disk + me_d

    ins = [
        pltpu.make_async_copy(a, b, in_sems.at[i])
        for i, (a, b) in enumerate(
            [(t_hbm, t_ref), (q_hbm, q_ref), (c_hbm, c_ref), (o_hbm, o_ref), (mol_hbm, mol_ref),
             (cond_hbm, cond_ref), (pf_hbm, pf_ref), (src_hbm, src_ref), (w_hbm, w_ref)]
        )
    ]
    for copy in ins:
        copy.start()

    barrier = pltpu.get_barrier_semaphore()

    def greet(i):
        peer = lax.rem(me + (i + 1), n)
        pl.semaphore_signal(
            barrier, inc=1, device_id=(peer // n_disk, lax.rem(peer, n_disk)), device_id_type=MESH
        )

    loop(n - 1, greet)

    for copy in ins[:4]:
        copy.wait()
    for h in range(2):
        for k in range(halves):
            cols = pl.ds(k * LANES, LANES)
            cloud = jnp.where(o_ref[h:h + 1, cols] == 1, c_ref[h, :, cols], 0.0)
            t2 = t_ref[h, :, cols] * t_ref[h, :, cols]
            fld[h, pl.ds(4 * k, 1), :] = t2 * t2
            fld[h, pl.ds(4 * k + 1, 1), :] = q_ref[h, :, cols]
            fld[h, pl.ds(4 * k + 2, 1), :] = cloud
            fld[h, pl.ds(4 * k + 3, 1), :] = cloud
    rows = 4 * halves
    lane = lax.broadcasted_iota(jnp.int32, (rows, LANES), 1)
    first_hour = (lane & block_cols) == 0
    turn = lax.rem(me_d, 2) * (2 * block_cols)
    f0 = fld[0]
    f1 = fld[1]
    for s in range(per):
        a = pltpu.roll(f0, lax.rem(turn + (LANES - s * block_cols), LANES), 1)
        b = pltpu.roll(f1, lax.rem(turn + (LANES + block_cols - s * block_cols), LANES), 1)
        p = jnp.where(first_hour, a, b)
        for k in range(halves):
            pk[k * per + s] = p[4 * k:4 * k + 4, :]

    pl.semaphore_wait(barrier, n - 1)

    def send(i):
        peer = lax.rem(me + (i + 1), n)
        ps = peer // n_disk
        pltpu.make_async_remote_copy(
            src_ref=pk.at[ps],
            dst_ref=recv.at[me],
            send_sem=send_sem,
            recv_sem=recv_sem,
            device_id=(ps, lax.rem(peer, n_disk)),
            device_id_type=MESH,
        ).start()

    loop(n - 1, send)
    recv[me] = pk[me_s]

    for copy in ins[4:]:
        copy.wait()
    g_lane = lax.broadcasted_iota(jnp.int32, (BANDS, BANDS * GPB), 1)
    g_band = lax.broadcasted_iota(jnp.int32, (BANDS, BANDS * GPB), 0)
    for j in range(GPB):
        m = mol_ref[pl.ds(j, BANDS, stride=GPB), :] * NEG_LOG2E
        for l in range(levels):
            mb[l, j] = jnp.broadcast_to(m[:, l:l + 1], (BANDS, LANES))
        hit = g_lane == g_band * GPB + j
        cv = jnp.sum(jnp.where(hit, cond_ref[...], 0.0), axis=1, keepdims=True) * NEG_LOG2E
        pv = jnp.sum(jnp.where(hit, pf_ref[...], 0.0), axis=1, keepdims=True)
        cb[j] = jnp.broadcast_to(cv, (BANDS, LANES))
        pb[j] = jnp.broadcast_to(pv, (BANDS, LANES))

    src = src_ref[...]
    place = lax.div(src, sector_cols) * block_cols + lax.rem(src, block_cols)
    w = w_ref[...]
    taps, pixels = w.shape
    row = lax.broadcasted_iota(jnp.int32, (block_cols, pixels), 0)
    for d in range(n_disk):
        acc = None
        for k in range(taps):
            term = jnp.where(row + d * block_cols == place[k:k + 1, :], w[k:k + 1, :], 0.0)
            acc = term if acc is None else acc + term
        hi = acc.astype(jnp.bfloat16)
        lo = (acc - hi.astype(jnp.float32)).astype(jnp.bfloat16)
        for h in range(2):
            at = pl.ds((2 * d + h) * block_cols, block_cols)
            whi[at, :] = hi
            wlo[at, :] = lo

    pltpu.make_async_remote_copy(
        src_ref=recv.at[pl.ds(0, n - 1)], dst_ref=recv.at[pl.ds(0, n - 1)],
        send_sem=send_sem, recv_sem=recv_sem, device_id=(me_s, me_d), device_id_type=MESH,
    ).wait_recv()

    left = lax.broadcasted_iota(jnp.int32, (4, LANES), 1) < 2 * block_cols
    lane16 = lax.broadcasted_iota(jnp.int32, (BANDS, LANES), 1)
    parts = []
    for pair in range(n_disk // 2):
        def fields(l):
            x = jnp.where(left, recv[l * n_disk + 2 * pair], recv[l * n_disk + 2 * pair + 1])
            return tuple(jnp.broadcast_to(x[f:f + 1, :], (8, LANES)) for f in range(3))

        if levels <= 8:
            held = [fields(l) for l in range(levels)]
        else:
            def fill(l):
                x = jnp.where(left, recv[l * n_disk + 2 * pair], recv[l * n_disk + 2 * pair + 1])
                sel[l] = x
            lax.fori_loop(0, levels, lambda l, _: (fill(l), 0)[1], 0)
        halves_out = []
        for half in range(BANDS // 8):
            at = pl.ds(8 * half, 8)
            total = None
            for j in range(GPB):
                cbj = cb[j, at, :]

                def step(l, carry):
                    depth, seen, emitted = carry
                    if levels <= 8:
                        b4, q, c = held[l]
                    else:
                        x = sel[l]
                        b4, q, c = x[0:1, :], x[1:2, :], x[2:3, :]
                    depth = depth + (mb[l, j, at, :] * q + cbj * c)
                    onward = jnp.exp2(depth)
                    emitted = emitted + b4 * (seen - onward)
                    return depth, onward, emitted

                zero = jnp.zeros((8, LANES), jnp.float32)
                carry = (zero, jnp.ones((8, LANES), jnp.float32), zero)
                if levels <= 8:
                    for l in range(levels):
                        carry = step(l, carry)
                    ground = held[levels - 1][0]
                else:
                    carry = lax.fori_loop(0, levels, step, carry)
                    ground = sel[levels - 1][0:1, :]
                got = pb[j, at, :] * (carry[2] + ground * carry[1])
                total = got if total is None else total + got
            halves_out.append(total)
        parts.append(jnp.concatenate(halves_out, axis=0) * (1.0 / GPB))

    hour = (lane16 & block_cols) != 0
    lhs = jnp.concatenate(
        [
            jnp.concatenate([jnp.where(hour == bool(h), r, 0.0) for r in parts], axis=1)
            for h in range(2)
        ],
        axis=0,
    ).astype(jnp.bfloat16)
    res = jnp.dot(lhs, whi[...], preferred_element_type=jnp.float32) + jnp.dot(
        lhs, wlo[...], preferred_element_type=jnp.float32
    )
    out_ref[0] = res[:BANDS]
    out_ref[1] = res[BANDS:]

    pltpu.make_async_remote_copy(
        src_ref=recv.at[pl.ds(0, n - 1)], dst_ref=recv.at[pl.ds(0, n - 1)],
        send_sem=send_sem, recv_sem=recv_sem, device_id=(me_s, me_d), device_id_type=MESH,
    ).wait_send()


def local(n_slab, n_disk, t, q, c, o, mol, cond, pf, src, w):
    hours, _, sector_cols = t.shape
    block_cols = sector_cols // n_slab
    taps, pixels = w.shape
    levels = mol.shape[1]
    n = n_slab * n_disk
    f32, bf16 = jnp.float32, jnp.bfloat16
    halves = sector_cols // LANES
    cond = cond.reshape(1, -1)
    pf = pf.reshape(1, -1)
    args = (t, q, c, o, mol, cond, pf, src, w)
    vmem = pltpu.VMEM
    return pl.pallas_call(
        functools.partial(kernel, n_slab, n_disk, sector_cols, block_cols),
        out_shape=jax.ShapeDtypeStruct((hours, BANDS, pixels), f32),
        in_specs=[pl.BlockSpec(memory_space=pl.ANY)] * len(args),
        out_specs=pl.BlockSpec(memory_space=pltpu.VMEM),
        scratch_shapes=[vmem(a.shape, a.dtype) for a in args]
        + [
            vmem((hours, 4 * halves, LANES), f32),
            vmem((n_slab, 4, LANES), f32),
            vmem((n, 4, LANES), f32),
            vmem((levels, 4, LANES), f32),
            vmem((levels, GPB, BANDS, LANES), f32),
            vmem((GPB, BANDS, LANES), f32),
            vmem((GPB, BANDS, LANES), f32),
            vmem((n_disk * 2 * block_cols, pixels), bf16),
            vmem((n_disk * 2 * block_cols, pixels), bf16),
            pltpu.SemaphoreType.DMA((len(args),)),
            pltpu.SemaphoreType.DMA,
            pltpu.SemaphoreType.DMA,
        ],
        compiler_params=pltpu.CompilerParams(
            collective_id=0, has_side_effects=True, vmem_limit_bytes=32 * 1024 * 1024
        ),
    )(*args)


def solution(mesh):
    in_specs = (
        P(None, "slab", "disk"),
        P(None, "slab", "disk"),
        P(None, "slab", "disk"),
        P(None, "disk"),
        P(),
        P(),
        P(),
        P(None, ("slab", "disk")),
        P(None, ("slab", "disk")),
    )
    out_specs = P(None, None, ("slab", "disk"))
    fn = functools.partial(local, mesh.shape["slab"], mesh.shape["disk"])
    return jax.shard_map(fn, mesh=mesh, in_specs=in_specs, out_specs=out_specs, check_vma=False)
```

```python
import functools

import jax
import jax.numpy as jnp
from jax import lax
from jax.experimental import pallas as pl
from jax.experimental.pallas import tpu as pltpu
from jax.sharding import PartitionSpec as P

BANDS = 16
GPB = 7
LANES = 128
MESH = pl.DeviceIdType.MESH
NEG_LOG2E = -1.4426950408889634


def loop(count, body):
    if count <= 64:
        for i in range(count):
            body(i)
    else:
        lax.fori_loop(0, count, lambda i, _: (body(i), 0)[1], 0)


def kernel(
    n_slab, n_disk, sector_cols, block_cols,
    t_hbm, q_hbm, c_hbm, o_hbm, mol_hbm, cond_hbm, pf_hbm, src_hbm, w_hbm,
    out_ref,
    t_ref, q_ref, c_ref, o_ref, mol_ref, cond_ref, pf_ref, src_ref, w_ref,
    fld, pk, recv, sel, cmat, ctr, mb, cb, pb, whi, wlo,
    in_sems, send_sem, recv_sem,
):
    n = n_slab * n_disk
    levels = n_slab
    halves = sector_cols // LANES
    per = LANES // block_cols
    me_s = lax.axis_index("slab")
    me_d = lax.axis_index("disk")
    me = me_s * n_disk + me_d

    ins = [
        pltpu.make_async_copy(a, b, in_sems.at[i])
        for i, (a, b) in enumerate(
            [(t_hbm, t_ref), (q_hbm, q_ref), (c_hbm, c_ref), (o_hbm, o_ref), (mol_hbm, mol_ref),
             (cond_hbm, cond_ref), (pf_hbm, pf_ref), (src_hbm, src_ref), (w_hbm, w_ref)]
        )
    ]
    for copy in ins[:4]:
        copy.start()

    barrier = pltpu.get_barrier_semaphore()

    def greet(i):
        peer = lax.rem(me + (i + 1), n)
        pl.semaphore_signal(
            barrier, inc=1, device_id=(peer // n_disk, lax.rem(peer, n_disk)), device_id_type=MESH
        )

    loop(n - 1, greet)
    for copy in ins[4:]:
        copy.start()

    for copy in ins[:4]:
        copy.wait()
    for h in range(2):
        for k in range(halves):
            cols = pl.ds(k * LANES, LANES)
            cloud = jnp.where(o_ref[h:h + 1, cols] == 1, c_ref[h, :, cols], 0.0)
            t2 = t_ref[h, :, cols] * t_ref[h, :, cols]
            fld[h, pl.ds(4 * k, 1), :] = t2 * t2
            fld[h, pl.ds(4 * k + 1, 1), :] = q_ref[h, :, cols]
            fld[h, pl.ds(4 * k + 2, 1), :] = cloud
            fld[h, pl.ds(4 * k + 3, 1), :] = cloud
    rows = 4 * halves
    lane = lax.broadcasted_iota(jnp.int32, (rows, LANES), 1)
    first_hour = (lane & block_cols) == 0
    turn = lax.rem(me_d, 2) * (2 * block_cols)
    f0 = fld[0]
    f1 = fld[1]
    for s in range(per):
        a = pltpu.roll(f0, lax.rem(turn + (LANES - s * block_cols), LANES), 1)
        b = pltpu.roll(f1, lax.rem(turn + (LANES + block_cols - s * block_cols), LANES), 1)
        p = jnp.where(first_hour, a, b)
        for k in range(halves):
            pk[k * per + s] = p[4 * k:4 * k + 4, :]

    pl.semaphore_wait(barrier, n - 1)

    def send(i):
        peer = lax.rem(me + (i + 1), n)
        ps = peer // n_disk
        pltpu.make_async_remote_copy(
            src_ref=pk.at[ps],
            dst_ref=recv.at[me],
            send_sem=send_sem,
            recv_sem=recv_sem,
            device_id=(ps, lax.rem(peer, n_disk)),
            device_id_type=MESH,
        ).start()

    loop(n - 1, send)
    recv[me] = pk[me_s]

    for copy in ins[4:]:
        copy.wait()
    gs = BANDS * GPB
    cmat[...] = jnp.zeros_like(cmat)
    cmat[pl.ds(0, levels), pl.ds(0, gs)] = mol_ref[...] * NEG_LOG2E
    cmat[pl.ds(levels, 1), pl.ds(0, gs)] = cond_ref[...] * NEG_LOG2E
    cmat[pl.ds(levels + 1, 1), pl.ds(0, gs)] = pf_ref[...]
    blocks, _, width = ctr.shape
    for k in range(blocks):
        ctr[k] = jnp.transpose(cmat[pl.ds(k * width, width), :])
    for j in range(GPB):
        m = [ctr[k, pl.ds(j, BANDS, stride=GPB), :] for k in range(blocks)]

        def column(l):
            at = l % width
            return jnp.broadcast_to(m[l // width][:, at:at + 1], (BANDS, LANES))

        for l in range(levels):
            mb[l, j] = column(l)
        cb[j] = column(levels)
        pb[j] = column(levels + 1)

    src = src_ref[...]
    place = lax.div(src, sector_cols) * block_cols + lax.rem(src, block_cols)
    w = w_ref[...]
    taps, pixels = w.shape
    row = lax.broadcasted_iota(jnp.int32, (block_cols, pixels), 0)
    for d in range(n_disk):
        acc = None
        for k in range(taps):
            term = jnp.where(row + d * block_cols == place[k:k + 1, :], w[k:k + 1, :], 0.0)
            acc = term if acc is None else acc + term
        hi = acc.astype(jnp.bfloat16)
        lo = (acc - hi.astype(jnp.float32)).astype(jnp.bfloat16)
        for h in range(2):
            at = pl.ds((2 * d + h) * block_cols, block_cols)
            whi[at, :] = hi
            wlo[at, :] = lo

    pltpu.make_async_remote_copy(
        src_ref=recv.at[pl.ds(0, n - 1)], dst_ref=recv.at[pl.ds(0, n - 1)],
        send_sem=send_sem, recv_sem=recv_sem, device_id=(me_s, me_d), device_id_type=MESH,
    ).wait_recv()

    left = lax.broadcasted_iota(jnp.int32, (4, LANES), 1) < 2 * block_cols
    lane16 = lax.broadcasted_iota(jnp.int32, (BANDS, LANES), 1)
    parts = []
    for pair in range(n_disk // 2):
        def fields(l):
            x = jnp.where(left, recv[l * n_disk + 2 * pair], recv[l * n_disk + 2 * pair + 1])
            return tuple(jnp.broadcast_to(x[f:f + 1, :], (8, LANES)) for f in range(3))

        if levels <= 8:
            held = [fields(l) for l in range(levels)]
        else:
            def fill(l):
                x = jnp.where(left, recv[l * n_disk + 2 * pair], recv[l * n_disk + 2 * pair + 1])
                sel[l] = x
            lax.fori_loop(0, levels, lambda l, _: (fill(l), 0)[1], 0)
        halves_out = []
        for half in range(BANDS // 8):
            at = pl.ds(8 * half, 8)
            total = None
            for j in range(GPB):
                cbj = cb[j, at, :]

                def step(l, carry):
                    depth, seen, emitted = carry
                    if levels <= 8:
                        b4, q, c = held[l]
                    else:
                        x = sel[l]
                        b4, q, c = x[0:1, :], x[1:2, :], x[2:3, :]
                    depth = depth + (mb[l, j, at, :] * q + cbj * c)
                    onward = jnp.exp2(depth)
                    emitted = emitted + b4 * (seen - onward)
                    return depth, onward, emitted

                zero = jnp.zeros((8, LANES), jnp.float32)
                carry = (zero, jnp.ones((8, LANES), jnp.float32), zero)
                if levels <= 8:
                    for l in range(levels):
                        carry = step(l, carry)
                    ground = held[levels - 1][0]
                else:
                    carry = lax.fori_loop(0, levels, step, carry)
                    ground = sel[levels - 1][0:1, :]
                got = pb[j, at, :] * (carry[2] + ground * carry[1])
                total = got if total is None else total + got
            halves_out.append(total)
        parts.append(jnp.concatenate(halves_out, axis=0) * (1.0 / GPB))

    hour = (lane16 & block_cols) != 0
    lhs = jnp.concatenate(
        [
            jnp.concatenate([jnp.where(hour == bool(h), r, 0.0) for r in parts], axis=1)
            for h in range(2)
        ],
        axis=0,
    ).astype(jnp.bfloat16)
    res = jnp.dot(lhs, whi[...], preferred_element_type=jnp.float32) + jnp.dot(
        lhs, wlo[...], preferred_element_type=jnp.float32
    )
    out_ref[0] = res[:BANDS]
    out_ref[1] = res[BANDS:]

    pltpu.make_async_remote_copy(
        src_ref=recv.at[pl.ds(0, n - 1)], dst_ref=recv.at[pl.ds(0, n - 1)],
        send_sem=send_sem, recv_sem=recv_sem, device_id=(me_s, me_d), device_id_type=MESH,
    ).wait_send()


def local(n_slab, n_disk, t, q, c, o, mol, cond, pf, src, w):
    hours, _, sector_cols = t.shape
    block_cols = sector_cols // n_slab
    taps, pixels = w.shape
    levels = mol.shape[1]
    mol = mol.T
    blocks = pl.cdiv(levels + 8, LANES)
    width = min(levels + 8, LANES)
    n = n_slab * n_disk
    f32, bf16 = jnp.float32, jnp.bfloat16
    halves = sector_cols // LANES
    cond = cond.reshape(1, -1)
    pf = pf.reshape(1, -1)
    args = (t, q, c, o, mol, cond, pf, src, w)
    vmem = pltpu.VMEM
    return pl.pallas_call(
        functools.partial(kernel, n_slab, n_disk, sector_cols, block_cols),
        out_shape=jax.ShapeDtypeStruct((hours, BANDS, pixels), f32),
        in_specs=[pl.BlockSpec(memory_space=pl.ANY)] * len(args),
        out_specs=pl.BlockSpec(memory_space=pltpu.VMEM),
        scratch_shapes=[vmem(a.shape, a.dtype) for a in args]
        + [
            vmem((hours, 4 * halves, LANES), f32),
            vmem((n_slab, 4, LANES), f32),
            vmem((n, 4, LANES), f32),
            vmem((levels, 4, LANES), f32),
            vmem((blocks * width, LANES), f32),
            vmem((blocks, LANES, width), f32),
            vmem((levels, GPB, BANDS, LANES), f32),
            vmem((GPB, BANDS, LANES), f32),
            vmem((GPB, BANDS, LANES), f32),
            vmem((n_disk * 2 * block_cols, pixels), bf16),
            vmem((n_disk * 2 * block_cols, pixels), bf16),
            pltpu.SemaphoreType.DMA((len(args),)),
            pltpu.SemaphoreType.DMA,
            pltpu.SemaphoreType.DMA,
        ],
        compiler_params=pltpu.CompilerParams(
            collective_id=0, has_side_effects=True, vmem_limit_bytes=60 * 1024 * 1024
        ),
    )(*args)


def solution(mesh):
    in_specs = (
        P(None, "slab", "disk"),
        P(None, "slab", "disk"),
        P(None, "slab", "disk"),
        P(None, "disk"),
        P(),
        P(),
        P(),
        P(None, ("slab", "disk")),
        P(None, ("slab", "disk")),
    )
    out_specs = P(None, None, ("slab", "disk"))
    fn = functools.partial(local, mesh.shape["slab"], mesh.shape["disk"])
    return jax.shard_map(fn, mesh=mesh, in_specs=in_specs, out_specs=out_specs, check_vma=False)
```

```python
import functools

import jax
import jax.numpy as jnp
from jax import lax
from jax.experimental import pallas as pl
from jax.experimental.pallas import tpu as pltpu
from jax.sharding import PartitionSpec as P

BANDS = 16
GPB = 7
LANES = 128
MESH = pl.DeviceIdType.MESH
NEG_LOG2E = -1.4426950408889634


def loop(count, body):
    if count <= 64:
        for i in range(count):
            body(i)
    else:
        lax.fori_loop(0, count, lambda i, _: (body(i), 0)[1], 0)


def kernel(
    n_slab, n_disk, sector_cols, block_cols,
    t_hbm, q_hbm, c_hbm, o_hbm, mol_hbm, cond_hbm, pf_hbm, src_hbm, w_hbm,
    out_ref,
    t_ref, q_ref, c_ref, o_ref, mol_ref, cond_ref, pf_ref, src_ref, w_ref,
    fld, pk, recv, rad, cmat, ctr, mb, cb, pb, wmat,
    in_sems, send_sem, recv_sem, rad_send, rad_recv,
):
    levels = n_slab
    halves = sector_cols // LANES
    per = LANES // block_cols
    me_s = lax.axis_index("slab")
    me_d = lax.axis_index("disk")

    def slab_peer(i):
        return lax.rem(me_s + (i + 1), n_slab)

    def disk_peer(i):
        return lax.rem(me_d + (i + 1), n_disk)

    ins = [
        pltpu.make_async_copy(a, b, in_sems.at[i])
        for i, (a, b) in enumerate(
            [(t_hbm, t_ref), (q_hbm, q_ref), (c_hbm, c_ref), (o_hbm, o_ref), (mol_hbm, mol_ref),
             (cond_hbm, cond_ref), (pf_hbm, pf_ref), (src_hbm, src_ref), (w_hbm, w_ref)]
        )
    ]
    for copy in ins[:4]:
        copy.start()

    barrier = pltpu.get_barrier_semaphore()

    def greet_slab(i):
        pl.semaphore_signal(barrier, inc=1, device_id=(slab_peer(i), me_d), device_id_type=MESH)

    def greet_disk(i):
        pl.semaphore_signal(barrier, inc=1, device_id=(me_s, disk_peer(i)), device_id_type=MESH)

    loop(n_slab - 1, greet_slab)
    loop(n_disk - 1, greet_disk)
    for copy in ins[4:]:
        copy.start()

    for copy in ins[:4]:
        copy.wait()
    for h in range(2):
        for k in range(halves):
            cols = pl.ds(k * LANES, LANES)
            cloud = jnp.where(o_ref[h:h + 1, cols] == 1, c_ref[h, :, cols], 0.0)
            t2 = t_ref[h, :, cols] * t_ref[h, :, cols]
            fld[h, pl.ds(4 * k, 1), :] = t2 * t2
            fld[h, pl.ds(4 * k + 1, 1), :] = q_ref[h, :, cols]
            fld[h, pl.ds(4 * k + 2, 1), :] = cloud
            fld[h, pl.ds(4 * k + 3, 1), :] = cloud
    rows = 4 * halves
    lane = lax.broadcasted_iota(jnp.int32, (rows, LANES), 1)
    odd = lax.rem(me_d, 2)
    f0 = fld[odd]
    f1 = fld[1 - odd]
    for s in range(per):
        x = pltpu.roll(f0, (LANES - s * block_cols) % LANES, 1) if s else f0
        y = pltpu.roll(f1, (LANES + block_cols - s * block_cols) % LANES, 1) if s != 1 else f1
        p = jnp.where((lane & block_cols) == 0, x, y)
        p = jnp.where(lane < LANES // 2, p, pltpu.roll(p, LANES // 2, 1))
        for k in range(halves):
            pk[k * per + s] = p[4 * k:4 * k + 4, :]

    pl.semaphore_wait(barrier, n_slab + n_disk - 2)

    def send(i):
        peer = slab_peer(i)
        pltpu.make_async_remote_copy(
            src_ref=pk.at[peer],
            dst_ref=recv.at[me_s],
            send_sem=send_sem,
            recv_sem=recv_sem,
            device_id=(peer, me_d),
            device_id_type=MESH,
        ).start()

    loop(n_slab - 1, send)
    recv[me_s] = pk[me_s]

    for copy in ins[4:]:
        copy.wait()
    gs = BANDS * GPB
    cmat[...] = jnp.zeros_like(cmat)
    cmat[pl.ds(0, levels), pl.ds(0, gs)] = mol_ref[...] * NEG_LOG2E
    cmat[pl.ds(levels, 1), pl.ds(0, gs)] = cond_ref[...] * NEG_LOG2E
    cmat[pl.ds(levels + 1, 1), pl.ds(0, gs)] = pf_ref[...] * (1.0 / GPB)
    blocks, _, width = ctr.shape
    for k in range(blocks):
        ctr[k] = jnp.transpose(cmat[pl.ds(k * width, width), :])
    lane8 = lax.broadcasted_iota(jnp.int32, (8, LANES), 1)
    group = lax.rem(lane8 // block_cols + (n_disk - me_d), n_disk)
    upper = group >= 2
    for j in range(GPB):
        m = [ctr[k, pl.ds(j, BANDS, stride=GPB), :] for k in range(blocks)]

        def column(l):
            at = l % width
            v = m[l // width][:, at:at + 1]
            return jnp.where(
                upper,
                jnp.broadcast_to(v[8:], (8, LANES)),
                jnp.broadcast_to(v[:8], (8, LANES)),
            )

        for l in range(levels):
            mb[l, j] = column(l)
        cb[j] = column(levels)
        pb[j] = column(levels + 1)

    src = src_ref[...]
    place = lax.div(src, sector_cols) * block_cols + lax.rem(src, block_cols)
    w = w_ref[...]
    taps, pixels = w.shape
    row = lax.broadcasted_iota(jnp.int32, (block_cols, pixels), 0)
    for d in range(n_disk):
        acc = None
        for k in range(taps):
            term = jnp.where(row + d * block_cols == place[k:k + 1, :], w[k:k + 1, :], 0.0)
            acc = term if acc is None else acc + term
        hi = acc.astype(jnp.bfloat16)
        wmat[pl.ds(d * block_cols, block_cols), :] = hi
        wmat[pl.ds(LANES + d * block_cols, block_cols), :] = (
            acc - hi.astype(jnp.float32)
        ).astype(jnp.bfloat16)

    levels_in = pltpu.make_async_remote_copy(
        src_ref=recv.at[pl.ds(0, n_slab - 1)], dst_ref=recv.at[pl.ds(0, n_slab - 1)],
        send_sem=send_sem, recv_sem=recv_sem, device_id=(me_s, me_d), device_id_type=MESH,
    )
    levels_in.wait_recv()

    def step(l, carry):
        x = recv[l]
        b4, q, c = (jnp.broadcast_to(x[f:f + 1, :], (8, LANES)) for f in range(3))
        out = []
        for j in range(GPB):
            depth, seen, emitted = carry[j]
            depth = depth + (mb[l, j] * q + cb[j] * c)
            onward = jnp.exp2(depth)
            emitted = emitted + b4 * (seen - onward)
            out.append((depth, onward, emitted))
        return tuple(out)

    zero = jnp.zeros((8, LANES), jnp.float32)
    carry = tuple((zero, jnp.ones((8, LANES), jnp.float32), zero) for _ in range(GPB))
    if levels <= 8:
        for l in range(levels):
            carry = step(l, carry)
    else:
        carry = lax.fori_loop(0, levels, step, carry)
    ground = jnp.broadcast_to(recv[levels - 1][0:1, :], (8, LANES))
    total = zero
    for j in range(GPB):
        total = total + pb[j] * (carry[j][2] + ground * carry[j][1])
    rad[me_d] = total

    def share(i):
        pltpu.make_async_remote_copy(
            src_ref=rad.at[me_d],
            dst_ref=rad.at[me_d],
            send_sem=rad_send,
            recv_sem=rad_recv,
            device_id=(me_s, disk_peer(i)),
            device_id_type=MESH,
        ).start()

    loop(n_disk - 1, share)
    rads_in = pltpu.make_async_remote_copy(
        src_ref=rad.at[pl.ds(0, n_disk - 1)], dst_ref=rad.at[pl.ds(0, n_disk - 1)],
        send_sem=rad_send, recv_sem=rad_recv, device_id=(me_s, me_d), device_id_type=MESH,
    )
    rads_in.wait_recv()

    block = lane8 // block_cols
    parts = [rad[d] for d in range(n_disk)]
    groups = []
    for g in range(4):
        x = parts[(0 - g) % n_disk]
        for b in range(1, n_disk):
            x = jnp.where(block == b, parts[(b - g) % n_disk], x)
        groups.append(pltpu.roll(x, (LANES - g * block_cols) % LANES, 1) if g else x)
    lhs = jnp.concatenate(groups, axis=0).astype(jnp.bfloat16)
    res = jnp.dot(
        jnp.concatenate([lhs, lhs], axis=1), wmat[...], preferred_element_type=jnp.float32
    )
    for g in range(4):
        out_ref[g % 2, pl.ds(8 * (g // 2), 8), :] = res[8 * g:8 * g + 8]

    levels_in.wait_send()
    rads_in.wait_send()


def local(n_slab, n_disk, t, q, c, o, mol, cond, pf, src, w):
    hours, _, sector_cols = t.shape
    block_cols = sector_cols // n_slab
    taps, pixels = w.shape
    levels = mol.shape[1]
    mol = mol.T
    blocks = pl.cdiv(levels + 8, LANES)
    width = min(levels + 8, LANES)
    f32, bf16 = jnp.float32, jnp.bfloat16
    halves = sector_cols // LANES
    assert hours == 2 and n_disk * block_cols == LANES and n_disk == 4
    cond = cond.reshape(1, -1)
    pf = pf.reshape(1, -1)
    args = (t, q, c, o, mol, cond, pf, src, w)
    vmem = pltpu.VMEM
    return pl.pallas_call(
        functools.partial(kernel, n_slab, n_disk, sector_cols, block_cols),
        out_shape=jax.ShapeDtypeStruct((hours, BANDS, pixels), f32),
        in_specs=[pl.BlockSpec(memory_space=pltpu.HBM)] * len(args),
        out_specs=pl.BlockSpec(memory_space=pltpu.VMEM),
        scratch_shapes=[vmem(a.shape, a.dtype) for a in args]
        + [
            vmem((hours, 4 * halves, LANES), f32),
            vmem((n_slab, 4, LANES), f32),
            vmem((n_slab, 4, LANES), f32),
            vmem((n_disk, 8, LANES), f32),
            vmem((blocks * width, LANES), f32),
            vmem((blocks, LANES, width), f32),
            vmem((levels, GPB, 8, LANES), f32),
            vmem((GPB, 8, LANES), f32),
            vmem((GPB, 8, LANES), f32),
            vmem((2 * LANES, pixels), bf16),
            pltpu.SemaphoreType.DMA((len(args),)),
            pltpu.SemaphoreType.DMA,
            pltpu.SemaphoreType.DMA,
            pltpu.SemaphoreType.DMA,
            pltpu.SemaphoreType.DMA,
        ],
        compiler_params=pltpu.CompilerParams(
            collective_id=0, has_side_effects=True, vmem_limit_bytes=32 * 1024 * 1024
        ),
    )(*args)


def solution(mesh):
    in_specs = (
        P(None, "slab", "disk"),
        P(None, "slab", "disk"),
        P(None, "slab", "disk"),
        P(None, "disk"),
        P(),
        P(),
        P(),
        P(None, ("slab", "disk")),
        P(None, ("slab", "disk")),
    )
    out_specs = P(None, None, ("slab", "disk"))
    fn = functools.partial(local, mesh.shape["slab"], mesh.shape["disk"])
    return jax.shard_map(fn, mesh=mesh, in_specs=in_specs, out_specs=out_specs, check_vma=False)
```

```python
import functools

import jax
import jax.numpy as jnp
from jax import lax
from jax.experimental import pallas as pl
from jax.experimental.pallas import tpu as pltpu
from jax.sharding import PartitionSpec as P

BANDS = 16
GPB = 7
LANES = 128
MESH = pl.DeviceIdType.MESH
NEG_LOG2E = -1.4426950408889634


def split(x):
    hi = x.astype(jnp.bfloat16).astype(jnp.float32)
    return hi, x - hi


def div(x, by):
    return x >> (by.bit_length() - 1) if by & (by - 1) == 0 else lax.div(x, by)


def rem(x, by):
    return x & (by - 1) if by & (by - 1) == 0 else lax.rem(x, by)


def kernel(
    n_slab, n_disk, sector_cols, block_cols,
    t_ref, q_ref, c_ref, o_ref, mol_ref, cond_ref, pf_ref, src_ref, w_ref,
    out_ref,
    fld, pk, recv, cmat, mmat, amat, fmat, bmat, smat, whi, wlo,
    send_sem, recv_sem,
):
    n = n_slab * n_disk
    levels = n_slab
    gs = BANDS * GPB
    halves = sector_cols // LANES
    per = LANES // block_cols
    me_s = lax.axis_index("slab")
    me_d = lax.axis_index("disk")
    me = me_s * n_disk + me_d

    barrier = pltpu.get_barrier_semaphore()

    def greet(i, carry):
        peer = rem(me + (i + 1), n)
        pl.semaphore_signal(
            barrier, inc=1, device_id=(div(peer, n_disk), rem(peer, n_disk)), device_id_type=MESH
        )
        return carry

    lax.fori_loop(0, n - 1, greet, 0)

    for h in range(2):
        for k in range(halves):
            cols = pl.ds(k * LANES, LANES)
            cloud = jnp.where(o_ref[h:h + 1, cols] == 1, c_ref[h, :, cols], 0.0)
            t2 = t_ref[h, :, cols] * t_ref[h, :, cols]
            fld[h, pl.ds(4 * k, 1), :] = t2 * t2
            fld[h, pl.ds(4 * k + 1, 1), :] = q_ref[h, :, cols]
            fld[h, pl.ds(4 * k + 2, 1), :] = cloud
            fld[h, pl.ds(4 * k + 3, 1), :] = cloud
    rows = 4 * halves
    lane = lax.broadcasted_iota(jnp.int32, (rows, LANES), 1)
    first_hour = (lane & block_cols) == 0
    turn = rem(me_d, 2) * (2 * block_cols)
    f0 = pltpu.roll(fld[0], turn, 1)
    f1 = pltpu.roll(fld[1], turn, 1)
    for s in range(per):
        x = pltpu.roll(f0, (LANES - s * block_cols) % LANES, 1) if s else f0
        y = pltpu.roll(f1, (LANES + block_cols - s * block_cols) % LANES, 1) if s != 1 else f1
        p = jnp.where(first_hour, x, y)
        for k in range(halves):
            pk[k * per + s] = p[4 * k:4 * k + 4, :]

    pl.semaphore_wait(barrier, n - 1)

    def send(i, carry):
        peer = rem(me + (i + 1), n)
        ps = div(peer, n_disk)
        pltpu.make_async_remote_copy(
            src_ref=pk.at[ps],
            dst_ref=recv.at[me],
            send_sem=send_sem,
            recv_sem=recv_sem,
            device_id=(ps, rem(peer, n_disk)),
            device_id_type=MESH,
        ).start()
        return carry

    lax.fori_loop(0, n - 1, send, 0)
    recv[me] = pk[me_s]

    mol_hi, mol_lo = split(jnp.transpose(mol_ref[...]) * NEG_LOG2E)
    cond_hi, cond_lo = split(cond_ref[...] * NEG_LOG2E)
    cmat[...] = jnp.zeros_like(cmat)
    for at, part in enumerate((mol_hi, cond_hi, mol_lo, cond_lo, mol_hi, cond_hi)):
        cmat[pl.ds(at * levels, levels), pl.ds(0, gs)] = jnp.broadcast_to(part, (levels, gs))
    mmat[...] = jnp.transpose(cmat[...])
    col = rem(lax.broadcasted_iota(jnp.int32, (gs, 6 * levels), 1), levels)

    def upto(l):
        return jnp.where(col <= l, mmat[pl.ds(0, gs), :], 0.0).astype(jnp.bfloat16)

    if levels <= 8:
        for l in range(levels):
            amat[l] = upto(l)

    g_lane = lax.broadcasted_iota(jnp.int32, (BANDS, gs), 1)
    g_band = lax.broadcasted_iota(jnp.int32, (BANDS, gs), 0) * GPB
    inside = (g_lane >= g_band) & (g_lane < g_band + GPB)
    s_hi, s_lo = split(jnp.where(inside, pf_ref[...] * (1.0 / GPB), 0.0))
    smat[pl.ds(0, BANDS), :] = s_hi.astype(jnp.bfloat16)
    smat[pl.ds(BANDS, BANDS), :] = s_lo.astype(jnp.bfloat16)

    src = src_ref[...]
    place = div(src, sector_cols) * block_cols + rem(src, block_cols)
    w = w_ref[...]
    taps, pixels = w.shape
    row = lax.broadcasted_iota(jnp.int32, (block_cols, pixels), 0)
    for d in range(n_disk):
        acc = None
        for k in range(taps):
            term = jnp.where(row + d * block_cols == place[k:k + 1, :], w[k:k + 1, :], 0.0)
            acc = term if acc is None else acc + term
        hi, lo = split(acc)
        hi = hi.astype(jnp.bfloat16)
        lo = lo.astype(jnp.bfloat16)
        for h in range(2):
            at = pl.ds((2 * d + h) * block_cols, block_cols)
            whi[at, :] = hi
            wlo[at, :] = lo

    arrive = pltpu.make_async_remote_copy(
        src_ref=recv.at[pl.ds(0, n - 1)], dst_ref=recv.at[pl.ds(0, n - 1)],
        send_sem=send_sem, recv_sem=recv_sem, device_id=(me_s, me_d), device_id_type=MESH,
    )
    arrive.wait_recv()

    left = lax.broadcasted_iota(jnp.int32, (4, LANES), 1) < 2 * block_cols
    for pair in range(n_disk // 2):
        cols = pl.ds(pair * LANES, LANES)

        def place_level(l, cols=cols, pair=pair):
            x = jnp.where(left, recv[l * n_disk + 2 * pair], recv[l * n_disk + 2 * pair + 1])
            bmat[pl.ds(l, 1), cols] = x[0:1, :]
            fmat[pl.ds(l, 1), cols] = x[1:2, :]
            fmat[pl.ds(levels + l, 1), cols] = x[2:3, :]

        for l in range(levels):
            place_level(l)
    f_hi, f_lo = split(fmat[...])
    fields = jnp.concatenate([f_hi, f_hi, f_lo], axis=0).astype(jnp.bfloat16)

    def step(l, a, carry):
        seen, emitted = carry
        onward = jnp.exp2(jnp.dot(a, fields, preferred_element_type=jnp.float32))
        return onward, emitted + bmat[pl.ds(l, 1), :] * (seen - onward)

    shape = (gs, fields.shape[1])
    carry = (jnp.ones(shape, jnp.float32), jnp.zeros(shape, jnp.float32))
    if levels <= 8:
        for l in range(levels):
            carry = step(l, amat[l], carry)
    else:
        carry = lax.fori_loop(0, levels, lambda l, c: step(l, upto(l), c), carry)
    e_hi, e_lo = split(carry[1] + bmat[pl.ds(levels - 1, 1), :] * carry[0])
    both = jnp.dot(smat[...], e_hi.astype(jnp.bfloat16), preferred_element_type=jnp.float32)
    rad = both[:BANDS] + both[BANDS:] + jnp.dot(
        smat[pl.ds(0, BANDS), :], e_lo.astype(jnp.bfloat16), preferred_element_type=jnp.float32
    )

    hour = (lax.broadcasted_iota(jnp.int32, rad.shape, 1) & block_cols) != 0
    lhs = jnp.concatenate([jnp.where(hour, 0.0, rad), jnp.where(hour, rad, 0.0)], axis=0)
    lhs = lhs.astype(jnp.bfloat16)
    res = jnp.dot(lhs, whi[...], preferred_element_type=jnp.float32) + jnp.dot(
        lhs, wlo[...], preferred_element_type=jnp.float32
    )
    out_ref[0] = res[:BANDS]
    out_ref[1] = res[BANDS:]
    arrive.wait_send()


def local(n_slab, n_disk, t, q, c, o, mol, cond, pf, src, w):
    hours, _, sector_cols = t.shape
    block_cols = sector_cols // n_slab
    taps, pixels = w.shape
    levels = mol.shape[1]
    n = n_slab * n_disk
    f32, bf16 = jnp.float32, jnp.bfloat16
    halves = sector_cols // LANES
    assert hours == 2 and n_disk * block_cols == LANES and n_disk == 4
    cond = cond.reshape(1, -1)
    pf = pf.reshape(1, -1)
    gs = BANDS * GPB
    kept = levels if levels <= 8 else 1
    args = (t, q, c, o, mol, cond, pf, src, w)
    vmem = pltpu.VMEM
    return pl.pallas_call(
        functools.partial(kernel, n_slab, n_disk, sector_cols, block_cols),
        out_shape=jax.ShapeDtypeStruct((hours, BANDS, pixels), f32),
        in_specs=[pl.BlockSpec(memory_space=pltpu.VMEM)] * len(args),
        out_specs=pl.BlockSpec(memory_space=pltpu.VMEM),
        scratch_shapes=[
            vmem((hours, 4 * halves, LANES), f32),
            vmem((n_slab, 4, LANES), f32),
            vmem((n, 4, LANES), f32),
            vmem((6 * levels, LANES), f32),
            vmem((LANES, 6 * levels), f32),
            vmem((kept, gs, 6 * levels), bf16),
            vmem((2 * levels, 2 * LANES), f32),
            vmem((levels, 2 * LANES), f32),
            vmem((2 * BANDS, gs), bf16),
            vmem((2 * LANES, pixels), bf16),
            vmem((2 * LANES, pixels), bf16),
            pltpu.SemaphoreType.DMA,
            pltpu.SemaphoreType.DMA,
        ],
        compiler_params=pltpu.CompilerParams(
            collective_id=0, has_side_effects=True, vmem_limit_bytes=32 * 1024 * 1024
        ),
    )(*args)


def solution(mesh):
    in_specs = (
        P(None, "slab", "disk"),
        P(None, "slab", "disk"),
        P(None, "slab", "disk"),
        P(None, "disk"),
        P(),
        P(),
        P(),
        P(None, ("slab", "disk")),
        P(None, ("slab", "disk")),
    )
    out_specs = P(None, None, ("slab", "disk"))
    fn = functools.partial(local, mesh.shape["slab"], mesh.shape["disk"])
    return jax.shard_map(fn, mesh=mesh, in_specs=in_specs, out_specs=out_specs, check_vma=False)
```

```python
import functools

import jax
import jax.numpy as jnp
from jax import lax
from jax.experimental import pallas as pl
from jax.experimental.pallas import tpu as pltpu
from jax.sharding import PartitionSpec as P

BANDS = 16
GPB = 7
LANES = 128
MESH = pl.DeviceIdType.MESH
NEG_LOG2E = -1.4426950408889634


def loop(count, body):
    if count <= 64:
        for i in range(count):
            body(i)
    else:
        lax.fori_loop(0, count, lambda i, _: (body(i), 0)[1], 0)


def split(x):
    hi = x.astype(jnp.bfloat16).astype(jnp.float32)
    return hi, x - hi


def div(x, by):
    return x >> (by.bit_length() - 1) if by & (by - 1) == 0 else lax.div(x, by)


def rem(x, by):
    return x & (by - 1) if by & (by - 1) == 0 else lax.rem(x, by)


def kernel(
    n_slab, n_disk, sector_cols, block_cols,
    t_ref, q_ref, c_ref, o_ref, mol_ref, cond_ref, pf_ref, src_ref, w_ref,
    out_ref,
    fld, pk, recv, radb, cmat, mmat, amat, fmat, bmat, smat, whi, wlo,
    send_sem, recv_sem, rad_send, rad_recv,
):
    levels = n_slab
    gs = BANDS * GPB
    halves = sector_cols // LANES
    per = LANES // block_cols
    me_s = lax.axis_index("slab")
    me_d = lax.axis_index("disk")

    def slab_peer(i):
        return rem(me_s + (i + 1), n_slab)

    def disk_peer(i):
        return rem(me_d + (i + 1), n_disk)

    barrier = pltpu.get_barrier_semaphore()

    def greet_slab(i):
        pl.semaphore_signal(barrier, inc=1, device_id=(slab_peer(i), me_d), device_id_type=MESH)

    def greet_disk(i):
        pl.semaphore_signal(barrier, inc=1, device_id=(me_s, disk_peer(i)), device_id_type=MESH)

    loop(n_slab - 1, greet_slab)
    loop(n_disk - 1, greet_disk)

    for h in range(2):
        for k in range(halves):
            cols = pl.ds(k * LANES, LANES)
            cloud = jnp.where(o_ref[h:h + 1, cols] == 1, c_ref[h, :, cols], 0.0)
            t2 = t_ref[h, :, cols] * t_ref[h, :, cols]
            fld[h, pl.ds(4 * k, 1), :] = t2 * t2
            fld[h, pl.ds(4 * k + 1, 1), :] = q_ref[h, :, cols]
            fld[h, pl.ds(4 * k + 2, 1), :] = cloud
            fld[h, pl.ds(4 * k + 3, 1), :] = cloud
    rows = 4 * halves
    lane = lax.broadcasted_iota(jnp.int32, (rows, LANES), 1)
    first_hour = (lane & block_cols) == 0
    turn = rem(me_d, 2) * (2 * block_cols)
    f0 = pltpu.roll(fld[0], turn, 1)
    f1 = pltpu.roll(fld[1], turn, 1)
    for s in range(per):
        x = pltpu.roll(f0, (LANES - s * block_cols) % LANES, 1) if s else f0
        y = pltpu.roll(f1, (LANES + block_cols - s * block_cols) % LANES, 1) if s != 1 else f1
        p = jnp.where(first_hour, x, y)
        for k in range(halves):
            pk[k * per + s] = p[4 * k:4 * k + 4, :]

    pl.semaphore_wait(barrier, n_slab + n_disk - 2)

    def send(i):
        peer = slab_peer(i)
        pltpu.make_async_remote_copy(
            src_ref=pk.at[peer],
            dst_ref=recv.at[me_s],
            send_sem=send_sem,
            recv_sem=recv_sem,
            device_id=(peer, me_d),
            device_id_type=MESH,
        ).start()

    loop(n_slab - 1, send)
    recv[me_s] = pk[me_s]

    mol_hi, mol_lo = split(jnp.transpose(mol_ref[...]) * NEG_LOG2E)
    cond_hi, cond_lo = split(cond_ref[...] * NEG_LOG2E)
    cmat[...] = jnp.zeros_like(cmat)
    for at, part in enumerate((mol_hi, cond_hi, mol_lo, cond_lo, mol_hi, cond_hi)):
        cmat[pl.ds(at * levels, levels), pl.ds(0, gs)] = jnp.broadcast_to(part, (levels, gs))
    mmat[...] = jnp.transpose(cmat[...])
    col = rem(lax.broadcasted_iota(jnp.int32, (gs, 6 * levels), 1), levels)

    def upto(l):
        return jnp.where(col <= l, mmat[pl.ds(0, gs), :], 0.0).astype(jnp.bfloat16)

    if levels <= 8:
        for l in range(levels):
            amat[l] = upto(l)

    g_lane = lax.broadcasted_iota(jnp.int32, (BANDS, gs), 1)
    g_band = lax.broadcasted_iota(jnp.int32, (BANDS, gs), 0) * GPB
    inside = (g_lane >= g_band) & (g_lane < g_band + GPB)
    s_hi, s_lo = split(jnp.where(inside, pf_ref[...] * (1.0 / GPB), 0.0))
    smat[pl.ds(0, BANDS), :] = s_hi.astype(jnp.bfloat16)
    smat[pl.ds(BANDS, BANDS), :] = s_lo.astype(jnp.bfloat16)

    arrive = pltpu.make_async_remote_copy(
        src_ref=recv.at[pl.ds(0, n_slab - 1)], dst_ref=recv.at[pl.ds(0, n_slab - 1)],
        send_sem=send_sem, recv_sem=recv_sem, device_id=(me_s, me_d), device_id_type=MESH,
    )
    arrive.wait_recv()

    for l in range(levels):
        x = recv[l]
        bmat[pl.ds(l, 1), :] = x[0:1, :]
        fmat[pl.ds(l, 1), :] = x[1:2, :]
        fmat[pl.ds(levels + l, 1), :] = x[2:3, :]
    f_hi, f_lo = split(fmat[...])
    fields = jnp.concatenate([f_hi, f_hi, f_lo], axis=0).astype(jnp.bfloat16)

    def step(l, a, carry):
        seen, emitted = carry
        onward = jnp.exp2(jnp.dot(a, fields, preferred_element_type=jnp.float32))
        return onward, emitted + bmat[pl.ds(l, 1), :] * (seen - onward)

    shape = (gs, fields.shape[1])
    carry = (jnp.ones(shape, jnp.float32), jnp.zeros(shape, jnp.float32))
    if levels <= 8:
        for l in range(levels):
            carry = step(l, amat[l], carry)
    else:
        carry = lax.fori_loop(0, levels, lambda l, c: step(l, upto(l), c), carry)
    e_hi, e_lo = split(carry[1] + bmat[pl.ds(levels - 1, 1), :] * carry[0])
    both = jnp.dot(smat[...], e_hi.astype(jnp.bfloat16), preferred_element_type=jnp.float32)
    mine = both[:BANDS] + both[BANDS:] + jnp.dot(
        smat[pl.ds(0, BANDS), :], e_lo.astype(jnp.bfloat16), preferred_element_type=jnp.float32
    )

    radb[me_d] = mine.astype(jnp.bfloat16)

    def share(i):
        pltpu.make_async_remote_copy(
            src_ref=radb.at[me_d],
            dst_ref=radb.at[me_d],
            send_sem=rad_send,
            recv_sem=rad_recv,
            device_id=(me_s, disk_peer(i)),
            device_id_type=MESH,
        ).start()

    loop(n_disk - 1, share)

    src = src_ref[...]
    place = div(src, sector_cols) * block_cols + rem(src, block_cols)
    w = w_ref[...]
    taps, pixels = w.shape
    row = lax.broadcasted_iota(jnp.int32, (block_cols, pixels), 0)
    for d in range(n_disk):
        acc = None
        for k in range(taps):
            term = jnp.where(row + d * block_cols == place[k:k + 1, :], w[k:k + 1, :], 0.0)
            acc = term if acc is None else acc + term
        hi, lo = split(acc)
        hi = hi.astype(jnp.bfloat16)
        lo = lo.astype(jnp.bfloat16)
        for h in range(2):
            at = pl.ds((2 * d + h) * block_cols, block_cols)
            whi[at, :] = hi
            wlo[at, :] = lo

    shared = pltpu.make_async_remote_copy(
        src_ref=radb.at[pl.ds(0, n_disk - 1)], dst_ref=radb.at[pl.ds(0, n_disk - 1)],
        send_sem=rad_send, recv_sem=rad_recv, device_id=(me_s, me_d), device_id_type=MESH,
    )
    shared.wait_recv()
    lane_out = lax.broadcasted_iota(jnp.int32, (BANDS, LANES), 1)
    left = lane_out < 2 * block_cols
    rad = jnp.concatenate(
        [
            jnp.where(
                left, radb[2 * pair].astype(jnp.float32), radb[2 * pair + 1].astype(jnp.float32)
            )
            for pair in range(n_disk // 2)
        ],
        axis=1,
    )
    hour = (lax.broadcasted_iota(jnp.int32, rad.shape, 1) & block_cols) != 0
    lhs = jnp.concatenate([jnp.where(hour, 0.0, rad), jnp.where(hour, rad, 0.0)], axis=0)
    lhs = lhs.astype(jnp.bfloat16)
    res = jnp.dot(lhs, whi[...], preferred_element_type=jnp.float32) + jnp.dot(
        lhs, wlo[...], preferred_element_type=jnp.float32
    )
    out_ref[0] = res[:BANDS]
    out_ref[1] = res[BANDS:]
    arrive.wait_send()
    shared.wait_send()


def local(n_slab, n_disk, t, q, c, o, mol, cond, pf, src, w):
    hours, _, sector_cols = t.shape
    block_cols = sector_cols // n_slab
    taps, pixels = w.shape
    levels = mol.shape[1]
    f32, bf16 = jnp.float32, jnp.bfloat16
    halves = sector_cols // LANES
    assert hours == 2 and n_disk * block_cols == LANES and n_disk == 4
    cond = cond.reshape(1, -1)
    pf = pf.reshape(1, -1)
    gs = BANDS * GPB
    kept = levels if levels <= 8 else 1
    args = (t, q, c, o, mol, cond, pf, src, w)
    vmem = pltpu.VMEM
    return pl.pallas_call(
        functools.partial(kernel, n_slab, n_disk, sector_cols, block_cols),
        out_shape=jax.ShapeDtypeStruct((hours, BANDS, pixels), f32),
        in_specs=[pl.BlockSpec(memory_space=pltpu.VMEM)] * len(args),
        out_specs=pl.BlockSpec(memory_space=pltpu.VMEM),
        scratch_shapes=[
            vmem((hours, 4 * halves, LANES), f32),
            vmem((n_slab, 4, LANES), f32),
            vmem((n_slab, 4, LANES), f32),
            vmem((n_disk, BANDS, LANES), bf16),
            vmem((6 * levels, LANES), f32),
            vmem((LANES, 6 * levels), f32),
            vmem((kept, gs, 6 * levels), bf16),
            vmem((2 * levels, LANES), f32),
            vmem((levels, LANES), f32),
            vmem((2 * BANDS, gs), bf16),
            vmem((2 * LANES, pixels), bf16),
            vmem((2 * LANES, pixels), bf16),
            pltpu.SemaphoreType.DMA,
            pltpu.SemaphoreType.DMA,
            pltpu.SemaphoreType.DMA,
            pltpu.SemaphoreType.DMA,
        ],
        compiler_params=pltpu.CompilerParams(
            collective_id=0, has_side_effects=True, vmem_limit_bytes=32 * 1024 * 1024
        ),
    )(*args)


def solution(mesh):
    in_specs = (
        P(None, "slab", "disk"),
        P(None, "slab", "disk"),
        P(None, "slab", "disk"),
        P(None, "disk"),
        P(),
        P(),
        P(),
        P(None, ("slab", "disk")),
        P(None, ("slab", "disk")),
    )
    out_specs = P(None, None, ("slab", "disk"))
    fn = functools.partial(local, mesh.shape["slab"], mesh.shape["disk"])
    return jax.shard_map(fn, mesh=mesh, in_specs=in_specs, out_specs=out_specs, check_vma=False)
```

```python
import functools

import jax
import jax.numpy as jnp
from jax import lax
from jax.experimental import pallas as pl
from jax.experimental.pallas import tpu as pltpu
from jax.sharding import PartitionSpec as P

BANDS = 16
GPB = 7
LANES = 128
MESH = pl.DeviceIdType.MESH
NEG_LOG2E = -1.4426950408889634


def split(x):
    hi = x.astype(jnp.bfloat16).astype(jnp.float32)
    return hi, x - hi


def div(x, by):
    return x >> (by.bit_length() - 1) if by & (by - 1) == 0 else lax.div(x, by)


def rem(x, by):
    return x & (by - 1) if by & (by - 1) == 0 else lax.rem(x, by)


def kernel(
    n_slab, n_disk, sector_cols, block_cols,
    t_ref, q_ref, c_ref, o_ref, mol_ref, cond_ref, pf_ref, src_ref, w_ref,
    out_ref,
    fld, pk, recv, cmat, mmat, amat, fmat, zmat, bmat, smat, whi, wlo,
    send_sem, recv_sem,
):
    n = n_slab * n_disk
    levels = n_slab
    gs = BANDS * GPB
    halves = sector_cols // LANES
    per = LANES // block_cols
    me_s = lax.axis_index("slab")
    me_d = lax.axis_index("disk")
    me = me_s * n_disk + me_d

    def partner(i):
        return me ^ (n - 1 - i) if n & (n - 1) == 0 else rem(me + (i + 1), n)

    barrier = pltpu.get_barrier_semaphore()

    def greet(i, carry):
        peer = partner(i)
        pl.semaphore_signal(
            barrier, inc=1, device_id=(div(peer, n_disk), rem(peer, n_disk)), device_id_type=MESH
        )
        return carry

    lax.fori_loop(0, n - 1, greet, 0)

    for h in range(2):
        for k in range(halves):
            cols = pl.ds(k * LANES, LANES)
            cloud = jnp.where(o_ref[h:h + 1, cols] == 1, c_ref[h, :, cols], 0.0)
            t2 = t_ref[h, :, cols] * t_ref[h, :, cols]
            vapour = q_ref[h, :, cols]
            fld[h, pl.ds(2 * k, 1), :] = t2 * t2
            fld[h, pl.ds(2 * k + 1, 1), :] = cloud
            fld[h, pl.ds(2 * (halves + k), 1), :] = vapour
            fld[h, pl.ds(2 * (halves + k) + 1, 1), :] = vapour
    rows = 4 * halves
    lane = lax.broadcasted_iota(jnp.int32, (rows, LANES), 1)
    first_hour = (lane & block_cols) == 0
    odd = rem(me_d, 2)
    turn = odd * (2 * block_cols)
    own = div(lane[:rows // 2], 2 * block_cols) == odd
    f0 = pltpu.roll(fld[0], turn, 1)
    f1 = pltpu.roll(fld[1], turn, 1)
    for s in range(per):
        x = pltpu.roll(f0, (LANES - s * block_cols) % LANES, 1) if s else f0
        y = pltpu.roll(f1, (LANES + block_cols - s * block_cols) % LANES, 1) if s != 1 else f1
        p = jnp.where(first_hour, x, y)
        p = jnp.where(own, p[:rows // 2], pltpu.roll(p[rows // 2:], LANES // 2, 1))
        for k in range(halves):
            pk[k * per + s] = p[2 * k:2 * k + 2, :]

    pl.semaphore_wait(barrier, n - 1)

    def send(i, carry):
        peer = partner(i)
        ps = div(peer, n_disk)
        pltpu.make_async_remote_copy(
            src_ref=pk.at[ps],
            dst_ref=recv.at[me],
            send_sem=send_sem,
            recv_sem=recv_sem,
            device_id=(ps, rem(peer, n_disk)),
            device_id_type=MESH,
        ).start()
        return carry

    lax.fori_loop(0, n - 1, send, 0)
    recv[me] = pk[me_s]

    mol_hi, mol_lo = split(jnp.transpose(mol_ref[...]) * NEG_LOG2E)
    cond_hi, cond_lo = split(cond_ref[...] * NEG_LOG2E)
    cmat[...] = jnp.zeros_like(cmat)
    for at, part in enumerate((mol_hi, cond_hi, mol_lo, cond_lo, mol_hi, cond_hi)):
        cmat[pl.ds(at * levels, levels), pl.ds(0, gs)] = jnp.broadcast_to(part, (levels, gs))
    mmat[...] = jnp.transpose(cmat[...])
    col = rem(lax.broadcasted_iota(jnp.int32, (gs, 6 * levels), 1), levels)

    def upto(l):
        return jnp.where(col <= l, mmat[pl.ds(0, gs), :], 0.0).astype(jnp.bfloat16)

    if levels <= 8:
        for l in range(levels):
            amat[l] = upto(l)

    g_lane = lax.broadcasted_iota(jnp.int32, (BANDS, gs), 1)
    g_band = lax.broadcasted_iota(jnp.int32, (BANDS, gs), 0) * GPB
    inside = (g_lane >= g_band) & (g_lane < g_band + GPB)
    s_hi, s_lo = split(jnp.where(inside, pf_ref[...] * (1.0 / GPB), 0.0))
    smat[pl.ds(0, BANDS), :] = s_hi.astype(jnp.bfloat16)
    smat[pl.ds(BANDS, BANDS), :] = s_lo.astype(jnp.bfloat16)

    src = src_ref[...]
    place = div(src, sector_cols) * block_cols + rem(src, block_cols)
    w = w_ref[...]
    taps, pixels = w.shape
    row = lax.broadcasted_iota(jnp.int32, (block_cols, pixels), 0)
    for d in range(n_disk):
        acc = None
        for k in range(taps):
            term = jnp.where(row + d * block_cols == place[k:k + 1, :], w[k:k + 1, :], 0.0)
            acc = term if acc is None else acc + term
        hi, lo = split(acc)
        hi = hi.astype(jnp.bfloat16)
        lo = lo.astype(jnp.bfloat16)
        for h in range(2):
            at = pl.ds((2 * d + h) * block_cols, block_cols)
            whi[at, :] = hi
            wlo[at, :] = lo

    arrive = pltpu.make_async_remote_copy(
        src_ref=recv.at[pl.ds(0, n - 1)], dst_ref=recv.at[pl.ds(0, n - 1)],
        send_sem=send_sem, recv_sem=recv_sem, device_id=(me_s, me_d), device_id_type=MESH,
    )
    arrive.wait_recv()

    left = lax.broadcasted_iota(jnp.int32, (2, LANES), 1) < 2 * block_cols
    for pair in range(n_disk // 2):
        cols = pl.ds(pair * LANES, LANES)
        for l in range(levels):
            even = recv[l * n_disk + 2 * pair]
            odds = recv[l * n_disk + 2 * pair + 1]
            x = jnp.where(left, even, odds)
            bmat[pl.ds(l, 1), cols] = x[0:1, :]
            fmat[pl.ds(levels + l, 1), cols] = x[1:2, :]
            zmat[pl.ds(l, 1), :] = jnp.where(left[0:1], odds[0:1], even[0:1])
        fmat[pl.ds(0, levels), cols] = pltpu.roll(zmat[...], LANES // 2, 1)
    f_hi, f_lo = split(fmat[...])
    fields = jnp.concatenate([f_hi, f_hi, f_lo], axis=0).astype(jnp.bfloat16)

    def step(l, a, carry):
        seen, emitted = carry
        onward = jnp.exp2(jnp.dot(a, fields, preferred_element_type=jnp.float32))
        return onward, emitted + bmat[pl.ds(l, 1), :] * (seen - onward)

    shape = (gs, fields.shape[1])
    carry = (jnp.ones(shape, jnp.float32), jnp.zeros(shape, jnp.float32))
    if levels <= 8:
        for l in range(levels):
            carry = step(l, amat[l], carry)
    else:
        carry = lax.fori_loop(0, levels, lambda l, c: step(l, upto(l), c), carry)
    e_hi, e_lo = split(carry[1] + bmat[pl.ds(levels - 1, 1), :] * carry[0])
    both = jnp.dot(smat[...], e_hi.astype(jnp.bfloat16), preferred_element_type=jnp.float32)
    rad = both[:BANDS] + both[BANDS:] + jnp.dot(
        smat[pl.ds(0, BANDS), :], e_lo.astype(jnp.bfloat16), preferred_element_type=jnp.float32
    )

    hour = (lax.broadcasted_iota(jnp.int32, rad.shape, 1) & block_cols) != 0
    lhs = jnp.concatenate([jnp.where(hour, 0.0, rad), jnp.where(hour, rad, 0.0)], axis=0)
    lhs = lhs.astype(jnp.bfloat16)
    res = jnp.dot(lhs, whi[...], preferred_element_type=jnp.float32) + jnp.dot(
        lhs, wlo[...], preferred_element_type=jnp.float32
    )
    out_ref[0] = res[:BANDS]
    out_ref[1] = res[BANDS:]
    arrive.wait_send()


def local(n_slab, n_disk, t, q, c, o, mol, cond, pf, src, w):
    hours, _, sector_cols = t.shape
    block_cols = sector_cols // n_slab
    taps, pixels = w.shape
    levels = mol.shape[1]
    n = n_slab * n_disk
    f32, bf16 = jnp.float32, jnp.bfloat16
    halves = sector_cols // LANES
    assert hours == 2 and n_disk * block_cols == LANES and n_disk == 4
    cond = cond.reshape(1, -1)
    pf = pf.reshape(1, -1)
    gs = BANDS * GPB
    kept = levels if levels <= 8 else 1
    args = (t, q, c, o, mol, cond, pf, src, w)
    vmem = pltpu.VMEM
    return pl.pallas_call(
        functools.partial(kernel, n_slab, n_disk, sector_cols, block_cols),
        out_shape=jax.ShapeDtypeStruct((hours, BANDS, pixels), f32),
        in_specs=[pl.BlockSpec(memory_space=pltpu.VMEM)] * len(args),
        out_specs=pl.BlockSpec(memory_space=pltpu.VMEM),
        scratch_shapes=[
            vmem((hours, 4 * halves, LANES), f32),
            vmem((n_slab, 2, LANES), f32),
            vmem((n, 2, LANES), f32),
            vmem((6 * levels, LANES), f32),
            vmem((LANES, 6 * levels), f32),
            vmem((kept, gs, 6 * levels), bf16),
            vmem((2 * levels, 2 * LANES), f32),
            vmem((levels, LANES), f32),
            vmem((levels, 2 * LANES), f32),
            vmem((2 * BANDS, gs), bf16),
            vmem((2 * LANES, pixels), bf16),
            vmem((2 * LANES, pixels), bf16),
            pltpu.SemaphoreType.DMA,
            pltpu.SemaphoreType.DMA,
        ],
        compiler_params=pltpu.CompilerParams(
            collective_id=0, has_side_effects=True, vmem_limit_bytes=32 * 1024 * 1024
        ),
    )(*args)


def solution(mesh):
    in_specs = (
        P(None, "slab", "disk"),
        P(None, "slab", "disk"),
        P(None, "slab", "disk"),
        P(None, "disk"),
        P(),
        P(),
        P(),
        P(None, ("slab", "disk")),
        P(None, ("slab", "disk")),
    )
    out_specs = P(None, None, ("slab", "disk"))
    fn = functools.partial(local, mesh.shape["slab"], mesh.shape["disk"])
    return jax.shard_map(fn, mesh=mesh, in_specs=in_specs, out_specs=out_specs, check_vma=False)
```

```python
import functools

import jax
import jax.numpy as jnp
from jax import lax
from jax.experimental import pallas as pl
from jax.experimental.pallas import tpu as pltpu
from jax.sharding import PartitionSpec as P

BANDS = 16
GPB = 7
LANES = 128
MESH = pl.DeviceIdType.MESH
NEG_LOG2E = -1.4426950408889634


def split(x):
    hi = x.astype(jnp.bfloat16).astype(jnp.float32)
    return hi, x - hi


def div(x, by):
    return x >> (by.bit_length() - 1) if by & (by - 1) == 0 else lax.div(x, by)


def rem(x, by):
    return x & (by - 1) if by & (by - 1) == 0 else lax.rem(x, by)


def kernel(
    n_slab, n_disk, sector_cols, block_cols,
    t_ref, q_ref, c_ref, o_ref, mol_ref, cond_ref, pf_ref, src_ref, w_ref,
    out_ref,
    fld, pk, recv, cmat, mmat, amat, fmat, zmat, bmat, smat, whi, wlo,
    send_sem, recv_sem,
):
    n = n_slab * n_disk
    levels = n_slab
    gs = BANDS * GPB
    halves = sector_cols // LANES
    per = LANES // block_cols
    me_s = lax.axis_index("slab")
    me_d = lax.axis_index("disk")
    me = me_s * n_disk + me_d

    def partner(i):
        return me ^ (n - 1 - i) if n & (n - 1) == 0 else rem(me + (i + 1), n)

    barrier = pltpu.get_barrier_semaphore()

    def greet(i, carry):
        peer = partner(i)
        pl.semaphore_signal(
            barrier, inc=1, device_id=(div(peer, n_disk), rem(peer, n_disk)), device_id_type=MESH
        )
        return carry

    lax.fori_loop(0, n - 1, greet, 0)

    for h in range(2):
        for k in range(halves):
            cols = pl.ds(k * LANES, LANES)
            cloud = jnp.where(o_ref[h:h + 1, cols] == 1, c_ref[h, :, cols], 0.0)
            t2 = t_ref[h, :, cols] * t_ref[h, :, cols]
            vapour = q_ref[h, :, cols]
            fld[h, pl.ds(2 * k, 1), :] = t2 * t2
            fld[h, pl.ds(2 * k + 1, 1), :] = cloud
            fld[h, pl.ds(2 * (halves + k), 1), :] = vapour
            fld[h, pl.ds(2 * (halves + k) + 1, 1), :] = vapour
    rows = 4 * halves
    lane = lax.broadcasted_iota(jnp.int32, (rows, LANES), 1)
    first_hour = (lane & block_cols) == 0
    odd = rem(me_d, 2)
    turn = odd * (2 * block_cols)
    own = div(lane[:rows // 2], 2 * block_cols) == odd
    f0 = pltpu.roll(fld[0], turn, 1)
    f1 = pltpu.roll(fld[1], turn, 1)
    for s in range(per):
        x = pltpu.roll(f0, (LANES - s * block_cols) % LANES, 1) if s else f0
        y = pltpu.roll(f1, (LANES + block_cols - s * block_cols) % LANES, 1) if s != 1 else f1
        p = jnp.where(first_hour, x, y)
        p = jnp.where(own, p[:rows // 2], pltpu.roll(p[rows // 2:], LANES // 2, 1))
        for k in range(halves):
            pk[k * per + s] = p[2 * k:2 * k + 2, :]

    mol_hi, mol_lo = split(jnp.transpose(mol_ref[...]) * NEG_LOG2E)
    cond_hi, cond_lo = split(cond_ref[...] * NEG_LOG2E)
    cmat[...] = jnp.zeros_like(cmat)
    for at, part in enumerate((mol_hi, cond_hi, mol_lo, cond_lo, mol_hi, cond_hi)):
        cmat[pl.ds(at * levels, levels), pl.ds(0, gs)] = jnp.broadcast_to(part, (levels, gs))
    mmat[...] = jnp.transpose(cmat[...])
    col = rem(lax.broadcasted_iota(jnp.int32, (gs, 6 * levels), 1), levels)

    def upto(l):
        return jnp.where(col <= l, mmat[pl.ds(0, gs), :], 0.0).astype(jnp.bfloat16)

    if levels <= 8:
        for l in range(levels):
            amat[l] = upto(l)

    g_lane = lax.broadcasted_iota(jnp.int32, (BANDS, gs), 1)
    g_band = lax.broadcasted_iota(jnp.int32, (BANDS, gs), 0) * GPB
    inside = (g_lane >= g_band) & (g_lane < g_band + GPB)
    s_hi, s_lo = split(jnp.where(inside, pf_ref[...] * (1.0 / GPB), 0.0))
    smat[pl.ds(0, BANDS), :] = s_hi.astype(jnp.bfloat16)
    smat[pl.ds(BANDS, BANDS), :] = s_lo.astype(jnp.bfloat16)

    pl.semaphore_wait(barrier, n - 1)

    def send(i, carry):
        peer = partner(i)
        ps = div(peer, n_disk)
        pltpu.make_async_remote_copy(
            src_ref=pk.at[ps],
            dst_ref=recv.at[me],
            send_sem=send_sem,
            recv_sem=recv_sem,
            device_id=(ps, rem(peer, n_disk)),
            device_id_type=MESH,
        ).start()
        return carry

    lax.fori_loop(0, n - 1, send, 0)
    recv[me] = pk[me_s]

    src = src_ref[...]
    place = div(src, sector_cols) * block_cols + rem(src, block_cols)
    w = w_ref[...]
    taps, pixels = w.shape
    row = lax.broadcasted_iota(jnp.int32, (block_cols, pixels), 0)
    for d in range(n_disk):
        acc = None
        for k in range(taps):
            term = jnp.where(row + d * block_cols == place[k:k + 1, :], w[k:k + 1, :], 0.0)
            acc = term if acc is None else acc + term
        hi, lo = split(acc)
        hi = hi.astype(jnp.bfloat16)
        lo = lo.astype(jnp.bfloat16)
        for h in range(2):
            at = pl.ds((2 * d + h) * block_cols, block_cols)
            whi[at, :] = hi
            wlo[at, :] = lo

    arrive = pltpu.make_async_remote_copy(
        src_ref=recv.at[pl.ds(0, n - 1)], dst_ref=recv.at[pl.ds(0, n - 1)],
        send_sem=send_sem, recv_sem=recv_sem, device_id=(me_s, me_d), device_id_type=MESH,
    )
    arrive.wait_recv()

    left = lax.broadcasted_iota(jnp.int32, (2, LANES), 1) < 2 * block_cols
    for pair in range(n_disk // 2):
        cols = pl.ds(pair * LANES, LANES)
        for l in range(levels):
            even = recv[l * n_disk + 2 * pair]
            odds = recv[l * n_disk + 2 * pair + 1]
            x = jnp.where(left, even, odds)
            bmat[pl.ds(l, 1), cols] = x[0:1, :]
            fmat[pl.ds(levels + l, 1), cols] = x[1:2, :]
            zmat[pl.ds(l, 1), :] = jnp.where(left[0:1], odds[0:1], even[0:1])
        fmat[pl.ds(0, levels), cols] = pltpu.roll(zmat[...], LANES // 2, 1)
    f_hi, f_lo = split(fmat[...])
    fields = jnp.concatenate([f_hi, f_hi, f_lo], axis=0).astype(jnp.bfloat16)

    def step(l, a, carry):
        seen, emitted = carry
        onward = jnp.exp2(jnp.dot(a, fields, preferred_element_type=jnp.float32))
        return onward, emitted + bmat[pl.ds(l, 1), :] * (seen - onward)

    shape = (gs, fields.shape[1])
    carry = (jnp.ones(shape, jnp.float32), jnp.zeros(shape, jnp.float32))
    if levels <= 8:
        for l in range(levels):
            carry = step(l, amat[l], carry)
    else:
        carry = lax.fori_loop(0, levels, lambda l, c: step(l, upto(l), c), carry)
    e_hi, e_lo = split(carry[1] + bmat[pl.ds(levels - 1, 1), :] * carry[0])
    both = jnp.dot(smat[...], e_hi.astype(jnp.bfloat16), preferred_element_type=jnp.float32)
    rad = both[:BANDS] + both[BANDS:] + jnp.dot(
        smat[pl.ds(0, BANDS), :], e_lo.astype(jnp.bfloat16), preferred_element_type=jnp.float32
    )

    hour = (lax.broadcasted_iota(jnp.int32, rad.shape, 1) & block_cols) != 0
    lhs = jnp.concatenate([jnp.where(hour, 0.0, rad), jnp.where(hour, rad, 0.0)], axis=0)
    lhs = lhs.astype(jnp.bfloat16)
    res = jnp.dot(lhs, whi[...], preferred_element_type=jnp.float32) + jnp.dot(
        lhs, wlo[...], preferred_element_type=jnp.float32
    )
    out_ref[0] = res[:BANDS]
    out_ref[1] = res[BANDS:]
    arrive.wait_send()


def local(n_slab, n_disk, t, q, c, o, mol, cond, pf, src, w):
    hours, _, sector_cols = t.shape
    block_cols = sector_cols // n_slab
    taps, pixels = w.shape
    levels = mol.shape[1]
    n = n_slab * n_disk
    f32, bf16 = jnp.float32, jnp.bfloat16
    halves = sector_cols // LANES
    assert hours == 2 and n_disk * block_cols == LANES and n_disk == 4
    cond = cond.reshape(1, -1)
    pf = pf.reshape(1, -1)
    gs = BANDS * GPB
    kept = levels if levels <= 8 else 1
    args = (t, q, c, o, mol, cond, pf, src, w)
    vmem = pltpu.VMEM
    return pl.pallas_call(
        functools.partial(kernel, n_slab, n_disk, sector_cols, block_cols),
        out_shape=jax.ShapeDtypeStruct((hours, BANDS, pixels), f32),
        in_specs=[pl.BlockSpec(memory_space=pltpu.VMEM)] * len(args),
        out_specs=pl.BlockSpec(memory_space=pltpu.VMEM),
        scratch_shapes=[
            vmem((hours, 4 * halves, LANES), f32),
            vmem((n_slab, 2, LANES), f32),
            vmem((n, 2, LANES), f32),
            vmem((6 * levels, LANES), f32),
            vmem((LANES, 6 * levels), f32),
            vmem((kept, gs, 6 * levels), bf16),
            vmem((2 * levels, 2 * LANES), f32),
            vmem((levels, LANES), f32),
            vmem((levels, 2 * LANES), f32),
            vmem((2 * BANDS, gs), bf16),
            vmem((2 * LANES, pixels), bf16),
            vmem((2 * LANES, pixels), bf16),
            pltpu.SemaphoreType.DMA,
            pltpu.SemaphoreType.DMA,
        ],
        compiler_params=pltpu.CompilerParams(
            collective_id=0, has_side_effects=True, vmem_limit_bytes=32 * 1024 * 1024
        ),
    )(*args)


def solution(mesh):
    in_specs = (
        P(None, "slab", "disk"),
        P(None, "slab", "disk"),
        P(None, "slab", "disk"),
        P(None, "disk"),
        P(),
        P(),
        P(),
        P(None, ("slab", "disk")),
        P(None, ("slab", "disk")),
    )
    out_specs = P(None, None, ("slab", "disk"))
    fn = functools.partial(local, mesh.shape["slab"], mesh.shape["disk"])
    return jax.shard_map(fn, mesh=mesh, in_specs=in_specs, out_specs=out_specs, check_vma=False)
```

```python
import functools

import jax
import jax.numpy as jnp
from jax import lax
from jax.experimental import pallas as pl
from jax.experimental.pallas import tpu as pltpu
from jax.sharding import PartitionSpec as P

BANDS = 16
GPB = 7
LANES = 128
MESH = pl.DeviceIdType.MESH
NEG_LOG2E = -1.4426950408889634


def split(x):
    hi = x.astype(jnp.bfloat16).astype(jnp.float32)
    return hi, x - hi


def div(x, by):
    return x >> (by.bit_length() - 1) if by & (by - 1) == 0 else lax.div(x, by)


def rem(x, by):
    return x & (by - 1) if by & (by - 1) == 0 else lax.rem(x, by)


def kernel(
    n_slab, n_disk, sector_cols, block_cols,
    t_ref, q_ref, c_ref, o_ref, mol_ref, cond_ref, pf_ref, src_ref, w_ref,
    out_ref,
    fld, pk, recv, mmat, amat, fmat, zmat, bmat, smat, whi, wlo,
    send_sem, recv_sem,
):
    n = n_slab * n_disk
    levels = n_slab
    gs = BANDS * GPB
    halves = sector_cols // LANES
    per = LANES // block_cols
    me_s = lax.axis_index("slab")
    me_d = lax.axis_index("disk")
    me = me_s * n_disk + me_d

    def partner(i):
        return rem(me + (i + 1), n)

    barrier = pltpu.get_barrier_semaphore()

    def greet(i, carry):
        peer = partner(i)
        pl.semaphore_signal(
            barrier, inc=1, device_id=(div(peer, n_disk), rem(peer, n_disk)), device_id_type=MESH
        )
        return carry

    lax.fori_loop(0, n - 1, greet, 0)

    for h in range(2):
        for k in range(halves):
            cols = pl.ds(k * LANES, LANES)
            cloud = jnp.where(o_ref[h:h + 1, cols] == 1, c_ref[h, :, cols], 0.0)
            t2 = t_ref[h, :, cols] * t_ref[h, :, cols]
            vapour = q_ref[h, :, cols]
            fld[h, pl.ds(2 * k, 1), :] = t2 * t2
            fld[h, pl.ds(2 * k + 1, 1), :] = cloud
            fld[h, pl.ds(2 * (halves + k), 1), :] = vapour
            fld[h, pl.ds(2 * (halves + k) + 1, 1), :] = vapour
    rows = 4 * halves
    lane = lax.broadcasted_iota(jnp.int32, (rows, LANES), 1)
    first_hour = (lane & block_cols) == 0
    odd = rem(me_d, 2)
    turn = odd * (2 * block_cols)
    own = div(lane[:rows // 2], 2 * block_cols) == odd
    f0 = pltpu.roll(fld[0], turn, 1)
    f1 = pltpu.roll(fld[1], turn, 1)
    for s in range(per):
        x = pltpu.roll(f0, (LANES - s * block_cols) % LANES, 1) if s else f0
        y = pltpu.roll(f1, (LANES + block_cols - s * block_cols) % LANES, 1) if s != 1 else f1
        p = jnp.where(first_hour, x, y)
        p = jnp.where(own, p[:rows // 2], pltpu.roll(p[rows // 2:], LANES // 2, 1))
        for k in range(halves):
            pk[k * per + s] = p[2 * k:2 * k + 2, :]

    g_lane = lax.broadcasted_iota(jnp.int32, (BANDS, gs), 1)
    g_band = lax.broadcasted_iota(jnp.int32, (BANDS, gs), 0) * GPB
    for j in range(GPB):
        at = pl.ds(j * BANDS, BANDS)
        hit = g_lane == g_band + j
        cond = jnp.sum(jnp.where(hit, cond_ref[...], 0.0), axis=1, keepdims=True) * NEG_LOG2E
        mol_hi, mol_lo = split(mol_ref[pl.ds(j, BANDS, stride=GPB), :] * NEG_LOG2E)
        cond_hi, cond_lo = split(jnp.broadcast_to(cond, (BANDS, levels)))
        for k, part in enumerate((mol_hi, cond_hi, mol_lo, cond_lo, mol_hi, cond_hi)):
            mmat[at, pl.ds(k * levels, levels)] = part
        pf = jnp.sum(jnp.where(hit, pf_ref[...], 0.0), axis=1, keepdims=True) * (1.0 / GPB)
        smat[at, :] = jnp.broadcast_to(pf, (BANDS, LANES))
    col = rem(lax.broadcasted_iota(jnp.int32, (gs, 6 * levels), 1), levels)

    def upto(l):
        return jnp.where(col <= l, mmat[pl.ds(0, gs), :], 0.0).astype(jnp.bfloat16)

    if levels <= 8:
        for l in range(levels):
            amat[l] = upto(l)

    pl.semaphore_wait(barrier, n - 1)

    def send(i, carry):
        peer = partner(i)
        ps = div(peer, n_disk)
        pltpu.make_async_remote_copy(
            src_ref=pk.at[ps],
            dst_ref=recv.at[me],
            send_sem=send_sem,
            recv_sem=recv_sem,
            device_id=(ps, rem(peer, n_disk)),
            device_id_type=MESH,
        ).start()
        return carry

    lax.fori_loop(0, n - 1, send, 0)
    recv[me] = pk[me_s]

    src = src_ref[...]
    place = div(src, sector_cols) * block_cols + rem(src, block_cols)
    w = w_ref[...]
    taps, pixels = w.shape
    row = lax.broadcasted_iota(jnp.int32, (block_cols, pixels), 0)
    for d in range(n_disk):
        acc = None
        for k in range(taps):
            term = jnp.where(row + d * block_cols == place[k:k + 1, :], w[k:k + 1, :], 0.0)
            acc = term if acc is None else acc + term
        hi, lo = split(acc)
        hi = hi.astype(jnp.bfloat16)
        lo = lo.astype(jnp.bfloat16)
        for h in range(2):
            at = pl.ds((2 * d + h) * block_cols, block_cols)
            whi[at, :] = hi
            wlo[at, :] = lo

    arrive = pltpu.make_async_remote_copy(
        src_ref=recv.at[pl.ds(0, n - 1)], dst_ref=recv.at[pl.ds(0, n - 1)],
        send_sem=send_sem, recv_sem=recv_sem, device_id=(me_s, me_d), device_id_type=MESH,
    )
    arrive.wait_recv()

    left = lax.broadcasted_iota(jnp.int32, (2, LANES), 1) < 2 * block_cols
    for pair in range(n_disk // 2):
        cols = pl.ds(pair * LANES, LANES)
        for l in range(levels):
            even = recv[l * n_disk + 2 * pair]
            odds = recv[l * n_disk + 2 * pair + 1]
            x = jnp.where(left, even, odds)
            bmat[pl.ds(l, 1), cols] = x[0:1, :]
            fmat[pl.ds(levels + l, 1), cols] = x[1:2, :]
            zmat[pl.ds(l, 1), :] = jnp.where(left[0:1], odds[0:1], even[0:1])
        fmat[pl.ds(0, levels), cols] = pltpu.roll(zmat[...], LANES // 2, 1)
    f_hi, f_lo = split(fmat[...])
    fields = jnp.concatenate([f_hi, f_hi, f_lo], axis=0).astype(jnp.bfloat16)

    def step(l, a, carry):
        seen, emitted = carry
        onward = jnp.exp2(jnp.dot(a, fields, preferred_element_type=jnp.float32))
        return onward, emitted + bmat[pl.ds(l, 1), :] * (seen - onward)

    shape = (gs, fields.shape[1])
    carry = (jnp.ones(shape, jnp.float32), jnp.zeros(shape, jnp.float32))
    if levels <= 8:
        for l in range(levels):
            carry = step(l, amat[l], carry)
    else:
        carry = lax.fori_loop(0, levels, lambda l, c: step(l, upto(l), c), carry)
    glow = carry[1] + bmat[pl.ds(levels - 1, 1), :] * carry[0]
    rad = None
    for j in range(GPB):
        at = slice(j * BANDS, (j + 1) * BANDS)
        weight = smat[pl.ds(j * BANDS, BANDS), :]
        term = jnp.concatenate([weight, weight], axis=1) * glow[at]
        rad = term if rad is None else rad + term

    hour = (lax.broadcasted_iota(jnp.int32, rad.shape, 1) & block_cols) != 0
    lhs = jnp.concatenate([jnp.where(hour, 0.0, rad), jnp.where(hour, rad, 0.0)], axis=0)
    lhs = lhs.astype(jnp.bfloat16)
    res = jnp.dot(lhs, whi[...], preferred_element_type=jnp.float32) + jnp.dot(
        lhs, wlo[...], preferred_element_type=jnp.float32
    )
    out_ref[0] = res[:BANDS]
    out_ref[1] = res[BANDS:]
    arrive.wait_send()


def local(n_slab, n_disk, t, q, c, o, mol, cond, pf, src, w):
    hours, _, sector_cols = t.shape
    block_cols = sector_cols // n_slab
    taps, pixels = w.shape
    levels = mol.shape[1]
    n = n_slab * n_disk
    f32, bf16 = jnp.float32, jnp.bfloat16
    halves = sector_cols // LANES
    assert hours == 2 and n_disk * block_cols == LANES and n_disk == 4
    cond = cond.reshape(1, -1)
    pf = pf.reshape(1, -1)
    gs = BANDS * GPB
    kept = levels if levels <= 8 else 1
    args = (t, q, c, o, mol, cond, pf, src, w)
    vmem = pltpu.VMEM
    return pl.pallas_call(
        functools.partial(kernel, n_slab, n_disk, sector_cols, block_cols),
        out_shape=jax.ShapeDtypeStruct((hours, BANDS, pixels), f32),
        in_specs=[pl.BlockSpec(memory_space=pltpu.VMEM)] * len(args),
        out_specs=pl.BlockSpec(memory_space=pltpu.VMEM),
        scratch_shapes=[
            vmem((hours, 4 * halves, LANES), f32),
            vmem((n_slab, 2, LANES), f32),
            vmem((n, 2, LANES), f32),
            vmem((gs, 6 * levels), f32),
            vmem((kept, gs, 6 * levels), bf16),
            vmem((2 * levels, 2 * LANES), f32),
            vmem((levels, LANES), f32),
            vmem((levels, 2 * LANES), f32),
            vmem((gs, LANES), f32),
            vmem((2 * LANES, pixels), bf16),
            vmem((2 * LANES, pixels), bf16),
            pltpu.SemaphoreType.DMA,
            pltpu.SemaphoreType.DMA,
        ],
        compiler_params=pltpu.CompilerParams(
            collective_id=0, has_side_effects=True, vmem_limit_bytes=32 * 1024 * 1024
        ),
    )(*args)


def solution(mesh):
    in_specs = (
        P(None, "slab", "disk"),
        P(None, "slab", "disk"),
        P(None, "slab", "disk"),
        P(None, "disk"),
        P(),
        P(),
        P(),
        P(None, ("slab", "disk")),
        P(None, ("slab", "disk")),
    )
    out_specs = P(None, None, ("slab", "disk"))
    fn = functools.partial(local, mesh.shape["slab"], mesh.shape["disk"])
    return jax.shard_map(fn, mesh=mesh, in_specs=in_specs, out_specs=out_specs, check_vma=False)
```

```python
import functools

import jax
import jax.numpy as jnp
from jax import lax
from jax.experimental import pallas as pl
from jax.experimental.pallas import tpu as pltpu
from jax.sharding import PartitionSpec as P

BANDS = 16
GPB = 7
LANES = 128
MESH = pl.DeviceIdType.MESH
NEG_LOG2E = -1.4426950408889634


def split(x):
    hi = x.astype(jnp.bfloat16).astype(jnp.float32)
    return hi, x - hi


def div(x, by):
    return x >> (by.bit_length() - 1) if by & (by - 1) == 0 else lax.div(x, by)


def rem(x, by):
    return x & (by - 1) if by & (by - 1) == 0 else lax.rem(x, by)


def kernel(
    n_slab, n_disk, sector_cols, block_cols,
    t_ref, q_ref, c_ref, o_ref, mol_ref, cond_ref, pf_ref, src_ref, w_ref,
    out_ref,
    fld, pk, recv, mmat, amat, fmat, zmat, bmat, smat, whi, wlo,
    send_sem, recv_sem,
):
    n = n_slab * n_disk
    levels = n_slab
    gs = BANDS * GPB
    halves = sector_cols // LANES
    per = LANES // block_cols
    me_s = lax.axis_index("slab")
    me_d = lax.axis_index("disk")
    me = me_s * n_disk + me_d

    def partner(i):
        return rem(me + (i + 1), n)

    barrier = pltpu.get_barrier_semaphore()

    def greet(i, carry):
        peer = partner(i)
        pl.semaphore_signal(
            barrier, inc=1, device_id=(div(peer, n_disk), rem(peer, n_disk)), device_id_type=MESH
        )
        return carry

    lax.fori_loop(0, n - 1, greet, 0)

    for h in range(2):
        for k in range(halves):
            cols = pl.ds(k * LANES, LANES)
            cloud = jnp.where(o_ref[h:h + 1, cols] == 1, c_ref[h, :, cols], 0.0)
            t2 = t_ref[h, :, cols] * t_ref[h, :, cols]
            vapour = q_ref[h, :, cols]
            fld[h, pl.ds(2 * k, 1), :] = t2 * t2
            fld[h, pl.ds(2 * k + 1, 1), :] = cloud
            fld[h, pl.ds(2 * (halves + k), 1), :] = vapour
            fld[h, pl.ds(2 * (halves + k) + 1, 1), :] = vapour
    rows = 4 * halves
    lane = lax.broadcasted_iota(jnp.int32, (rows, LANES), 1)
    first_hour = (lane & block_cols) == 0
    odd = rem(me_d, 2)
    turn = odd * (2 * block_cols)
    own = div(lane[:rows // 2], 2 * block_cols) == odd
    f0 = pltpu.roll(fld[0], turn, 1)
    f1 = pltpu.roll(fld[1], turn, 1)
    for s in range(per):
        x = pltpu.roll(f0, (LANES - s * block_cols) % LANES, 1) if s else f0
        y = pltpu.roll(f1, (LANES + block_cols - s * block_cols) % LANES, 1) if s != 1 else f1
        p = jnp.where(first_hour, x, y)
        p = jnp.where(own, p[:rows // 2], pltpu.roll(p[rows // 2:], LANES // 2, 1))
        for k in range(halves):
            pk[k * per + s] = p[2 * k:2 * k + 2, :]

    g_lane = lax.broadcasted_iota(jnp.int32, (BANDS, gs), 1)
    g_band = lax.broadcasted_iota(jnp.int32, (BANDS, gs), 0) * GPB
    for j in range(GPB):
        at = pl.ds(j * BANDS, BANDS)
        hit = g_lane == g_band + j
        cond = jnp.sum(jnp.where(hit, cond_ref[...], 0.0), axis=1, keepdims=True) * NEG_LOG2E
        mol_hi, mol_lo = split(mol_ref[pl.ds(j, BANDS, stride=GPB), :] * NEG_LOG2E)
        cond_hi, cond_lo = split(jnp.broadcast_to(cond, (BANDS, levels)))
        for k, part in enumerate((mol_hi, cond_hi, mol_lo, cond_lo, mol_hi, cond_hi)):
            mmat[at, pl.ds(k * levels, levels)] = part
        pf = jnp.sum(jnp.where(hit, pf_ref[...], 0.0), axis=1, keepdims=True) * (1.0 / GPB)
        smat[at, :] = jnp.broadcast_to(pf, (BANDS, LANES))
    col = rem(lax.broadcasted_iota(jnp.int32, (gs, 6 * levels), 1), levels)

    def upto(l):
        return jnp.where(col <= l, mmat[pl.ds(0, gs), :], 0.0).astype(jnp.bfloat16)

    if levels <= 8:
        for l in range(levels):
            amat[pl.ds(l * gs, gs), :] = upto(l)

    pl.semaphore_wait(barrier, n - 1)

    def send(i, carry):
        peer = partner(i)
        ps = div(peer, n_disk)
        pltpu.make_async_remote_copy(
            src_ref=pk.at[ps],
            dst_ref=recv.at[me],
            send_sem=send_sem,
            recv_sem=recv_sem,
            device_id=(ps, rem(peer, n_disk)),
            device_id_type=MESH,
        ).start()
        return carry

    lax.fori_loop(0, n - 1, send, 0)
    recv[me] = pk[me_s]

    src = src_ref[...]
    place = div(src, sector_cols) * block_cols + rem(src, block_cols)
    w = w_ref[...]
    taps, pixels = w.shape
    row = lax.broadcasted_iota(jnp.int32, (block_cols, pixels), 0)
    for d in range(n_disk):
        acc = None
        for k in range(taps):
            term = jnp.where(row + d * block_cols == place[k:k + 1, :], w[k:k + 1, :], 0.0)
            acc = term if acc is None else acc + term
        hi, lo = split(acc)
        hi = hi.astype(jnp.bfloat16)
        lo = lo.astype(jnp.bfloat16)
        for h in range(2):
            at = pl.ds((2 * d + h) * block_cols, block_cols)
            whi[at, :] = hi
            wlo[at, :] = lo

    arrive = pltpu.make_async_remote_copy(
        src_ref=recv.at[pl.ds(0, n - 1)], dst_ref=recv.at[pl.ds(0, n - 1)],
        send_sem=send_sem, recv_sem=recv_sem, device_id=(me_s, me_d), device_id_type=MESH,
    )
    arrive.wait_recv()

    left = lax.broadcasted_iota(jnp.int32, (2, LANES), 1) < 2 * block_cols
    for pair in range(n_disk // 2):
        cols = pl.ds(pair * LANES, LANES)
        for l in range(levels):
            even = recv[l * n_disk + 2 * pair]
            odds = recv[l * n_disk + 2 * pair + 1]
            x = jnp.where(left, even, odds)
            bmat[pl.ds(l, 1), cols] = x[0:1, :]
            fmat[pl.ds(levels + l, 1), cols] = x[1:2, :]
            zmat[pl.ds(l, 1), :] = jnp.where(left[0:1], odds[0:1], even[0:1])
        fmat[pl.ds(0, levels), cols] = pltpu.roll(zmat[...], LANES // 2, 1)
    f_hi, f_lo = split(fmat[...])
    fields = jnp.concatenate([f_hi, f_hi, f_lo], axis=0).astype(jnp.bfloat16)

    def step(l, depth, carry):
        seen, emitted = carry
        onward = jnp.exp2(depth)
        return onward, emitted + bmat[pl.ds(l, 1), :] * (seen - onward)

    shape = (gs, fields.shape[1])
    carry = (jnp.ones(shape, jnp.float32), jnp.zeros(shape, jnp.float32))
    if levels <= 8:
        depths = jnp.dot(amat[...], fields, preferred_element_type=jnp.float32)
        for l in range(levels):
            carry = step(l, depths[l * gs:(l + 1) * gs], carry)
    else:
        carry = lax.fori_loop(0, levels, lambda l, c: step(l, jnp.dot(upto(l), fields, preferred_element_type=jnp.float32), c), carry)
    glow = carry[1] + bmat[pl.ds(levels - 1, 1), :] * carry[0]
    rad = None
    for j in range(GPB):
        at = slice(j * BANDS, (j + 1) * BANDS)
        weight = smat[pl.ds(j * BANDS, BANDS), :]
        term = jnp.concatenate([weight, weight], axis=1) * glow[at]
        rad = term if rad is None else rad + term

    hour = (lax.broadcasted_iota(jnp.int32, rad.shape, 1) & block_cols) != 0
    lhs = jnp.concatenate([jnp.where(hour, 0.0, rad), jnp.where(hour, rad, 0.0)], axis=0)
    lhs = lhs.astype(jnp.bfloat16)
    res = jnp.dot(lhs, whi[...], preferred_element_type=jnp.float32) + jnp.dot(
        lhs, wlo[...], preferred_element_type=jnp.float32
    )
    out_ref[0] = res[:BANDS]
    out_ref[1] = res[BANDS:]
    arrive.wait_send()


def local(n_slab, n_disk, t, q, c, o, mol, cond, pf, src, w):
    hours, _, sector_cols = t.shape
    block_cols = sector_cols // n_slab
    taps, pixels = w.shape
    levels = mol.shape[1]
    n = n_slab * n_disk
    f32, bf16 = jnp.float32, jnp.bfloat16
    halves = sector_cols // LANES
    assert hours == 2 and n_disk * block_cols == LANES and n_disk == 4
    cond = cond.reshape(1, -1)
    pf = pf.reshape(1, -1)
    gs = BANDS * GPB
    kept = levels if levels <= 8 else 1
    args = (t, q, c, o, mol, cond, pf, src, w)
    vmem = pltpu.VMEM
    return pl.pallas_call(
        functools.partial(kernel, n_slab, n_disk, sector_cols, block_cols),
        out_shape=jax.ShapeDtypeStruct((hours, BANDS, pixels), f32),
        in_specs=[pl.BlockSpec(memory_space=pltpu.VMEM)] * len(args),
        out_specs=pl.BlockSpec(memory_space=pltpu.VMEM),
        scratch_shapes=[
            vmem((hours, 4 * halves, LANES), f32),
            vmem((n_slab, 2, LANES), f32),
            vmem((n, 2, LANES), f32),
            vmem((gs, 6 * levels), f32),
            vmem((kept * gs, 6 * levels), bf16),
            vmem((2 * levels, 2 * LANES), f32),
            vmem((levels, LANES), f32),
            vmem((levels, 2 * LANES), f32),
            vmem((gs, LANES), f32),
            vmem((2 * LANES, pixels), bf16),
            vmem((2 * LANES, pixels), bf16),
            pltpu.SemaphoreType.DMA,
            pltpu.SemaphoreType.DMA,
        ],
        compiler_params=pltpu.CompilerParams(
            collective_id=0, has_side_effects=True, vmem_limit_bytes=32 * 1024 * 1024
        ),
    )(*args)


def solution(mesh):
    in_specs = (
        P(None, "slab", "disk"),
        P(None, "slab", "disk"),
        P(None, "slab", "disk"),
        P(None, "disk"),
        P(),
        P(),
        P(),
        P(None, ("slab", "disk")),
        P(None, ("slab", "disk")),
    )
    out_specs = P(None, None, ("slab", "disk"))
    fn = functools.partial(local, mesh.shape["slab"], mesh.shape["disk"])
    return jax.shard_map(fn, mesh=mesh, in_specs=in_specs, out_specs=out_specs, check_vma=False)
```
